512 devices in a mesh: dp: 64 (over y, x, core), tensor: 8 (over z).
Axes of the slice: x: 4, y: 8, z: 8, core: 2. Of those that a mesh axis runs over, the one named last changes fastest.
Arguments:
- tokens: bfloat16 [32768, 6144], P('dp', 'tensor'), may hold values from -6 to 6
- old_master: float32 [6144, 7168], P('dp', 'tensor'), may hold values from -0.078125 to 0.078125
- old_first: float32 [6144, 7168], P('dp', 'tensor'), may hold values from -4 to 4
- old_second: float32 [6144, 7168], P('dp', 'tensor'), may hold values from 0.01 to 1
- piece_lengths: int32 [64], replicated, may hold values from 1 to 15, 672 in all
- piece_shifts: int32 [64], replicated, may hold values from 0 to 63, each once
Outputs:
- new_master: float32 [6144, 7168], P('dp', 'tensor')
- new_first: float32 [6144, 7168], P('dp', 'tensor')
- new_second: float32 [6144, 7168], P('dp', 'tensor')
- query: bfloat16 [32768, 6144], P('dp', 'tensor')
- key: bfloat16 [32768, 1024], P('dp', 'tensor')
The draws below stay inside these ranges and needn't reach their ends.
Inputs may be any that keep to these rules, and one draw needn't show every extreme that they name: `piece_lengths`: they sum to 672, and the longest is exactly 15. `piece_shifts`: each of 0 to 63 appears once.
All inputs are finite; a program needn't handle non-finite values.
Results may differ from the reference program's by a relative error of at most 0.0065.
Values may be sent and summed in bfloat16 or wider, within the bound.
No kernel may reach another device: no remote copies, remote signals or barrier semaphores. Data moves between devices by JAX's collectives and lax.ppermute only.
A program may use at most 128 MiB of HBM per device.

```python
import math
import jax
import jax.numpy as jnp
import numpy as np

D = 6144
HQ = 48
HK = 8
HS = 128
TOKENS = 32768
COLS = 7168
HQ_DEV = 6
HEADS_DEV = 7
D_DEV = 96
ROWS_DEV = 672
MOST = 15
N_DP = 64
N_TENSOR = 8


def block_levels(own_key, dims, cuts, smallest, largest):
    level = 1.0
    for position, parts in cuts:
        steps = jax.random.uniform(jax.random.fold_in(jax.random.fold_in(own_key, 6), position), (parts,), jnp.float32, smallest / len(cuts), largest / len(cuts))
        level = level * jnp.repeat(jnp.exp(steps), dims[position] // parts).reshape((-1,) + (1,) * (len(dims) - 1 - position))
    return level


def length_profile(count, total, most, lean):
    portions = [(1 << 20) // math.isqrt(standing ** lean) + 1 for standing in range(2, count + 1)]
    spare, given = total - most - (count - 1), [1] * (count - 1)
    while spare > 0:
        free = [i for i in range(count - 1) if given[i] < most]
        mass, remaining = sum([portions[i] for i in free]), spare
        for i in free:
            addition = min(most - given[i], max(1, remaining * portions[i] // mass), spare)
            given[i] = given[i] + addition
            spare = spare - addition
    return np.array([most] + given)


def ragged_sizes(rng, amount, total, bound, lean):
    if amount == 2:
        one = jax.random.randint(rng, (), max(1, total - bound), min(bound, total - 1) + 1)
        return jnp.stack([one, total - one])
    sizes = jnp.asarray(length_profile(amount, total, bound, lean), jnp.int32)
    pairs = (amount - 1) // 2
    donor, receiver = sizes[1:1 + 2 * pairs:2], sizes[2:2 + 2 * pairs:2]
    margin = jnp.minimum(donor - 1, bound - receiver)
    shifted = jax.random.randint(jax.random.fold_in(rng, 1), (pairs,), 0, 1 << 20) % (margin + 1)
    sizes = sizes.at[1:1 + 2 * pairs:2].set(donor - shifted).at[2:2 + 2 * pairs:2].set(receiver + shifted)
    return sizes[jax.random.permutation(jax.random.fold_in(rng, 2), amount)]


def gaussian(own_key, extent, scale, limit, shards=(), kind=jnp.bfloat16):
    result = jax.random.normal(own_key, extent, jnp.float32) * scale
    if len(shards) > 0:
        result = block_levels(own_key, extent, shards, -0.22, 0.18) * result
    return jnp.clip(result, min=-limit, max=limit).astype(kind)


def setup_inputs(seed: int = 0) -> dict:
    streams_of = jax.random.split(jax.random.key(seed), 7)
    tokens = gaussian(streams_of[0], (TOKENS, D), 1.0, 6.0, ((0, 64), (1, 8)))
    old_master = gaussian(streams_of[1], (D, COLS), D ** -0.5, 0.078125, ((0, 64), (1, 8)), jnp.float32)
    old_first = gaussian(streams_of[2], (D, COLS), 0.5, 4.0, ((0, 64), (1, 8)), jnp.float32)
    old_second = jnp.clip(jnp.exp(math.log(1.0) - 4.6051702 * jax.random.uniform(streams_of[3], (D, COLS), jnp.float32) ** block_levels(streams_of[3], (D, COLS), ((0, 64), (1, 8)), -0.2, 0.2)), 0.01, 1.0)
    piece_lengths = ragged_sizes(streams_of[4], N_DP, ROWS_DEV, MOST, 2).astype(jnp.int32)
    piece_shifts = jax.random.permutation(streams_of[5], N_DP).astype(jnp.int32)
    return {"tokens": tokens, "old_master": old_master, "old_first": old_first, "old_second": old_second, "piece_lengths": piece_lengths, "piece_shifts": piece_shifts}


def regroup(state):
    shaped = state.reshape(N_DP, D_DEV, N_TENSOR, HEADS_DEV, HS)
    return shaped.transpose(2, 0, 1, 3, 4).reshape(N_TENSOR, N_DP, ROWS_DEV, HS)


def ungroup(grouped):
    shaped = grouped.reshape(N_TENSOR, N_DP, D_DEV, HEADS_DEV, HS)
    return shaped.transpose(1, 2, 0, 3, 4).reshape(D, COLS)


def reference(tokens, old_master, old_first, old_second, piece_lengths, piece_shifts):
    slot_ids = jnp.arange(ROWS_DEV, dtype=jnp.int32)
    seg_ends = jnp.cumsum(piece_lengths).astype(jnp.int32)
    segment = jnp.sum((slot_ids[:, None] >= seg_ends[None, :]).astype(jnp.int32), axis=1).astype(jnp.int32)
    slot_shift = piece_shifts[segment].astype(jnp.int32)
    owners = jnp.arange(N_DP, dtype=jnp.int32)
    source = ((owners[:, None] - slot_shift[None, :]) % N_DP).astype(jnp.int32)

    def move(state):
        grouped = regroup(state)
        return ungroup(grouped[:, source, slot_ids[None, :]])

    new_master = move(old_master)
    new_first = move(old_first)
    new_second = move(old_second)
    weights = new_master.astype(jnp.bfloat16)
    product = jnp.dot(tokens, weights, preferred_element_type=jnp.float32)
    blocks = product.reshape(TOKENS, N_TENSOR, HEADS_DEV * HS)
    query = blocks[:, :, :HQ_DEV * HS].reshape(TOKENS, HQ * HS).astype(jnp.bfloat16)
    key = blocks[:, :, HQ_DEV * HS:].reshape(TOKENS, HK * HS).astype(jnp.bfloat16)
    return new_master, new_first, new_second, query, key
```

```python
import functools

import jax
import jax.numpy as jnp
from jax import lax
from jax.experimental import pallas as pl
from jax.experimental.pallas import tpu as pltpu
from jax.sharding import PartitionSpec as P

HQ = 48
HS = 128
NX = 4
NC = 2
HEADS = 7
ROWS = 96
SLOTS = ROWS * HEADS
HALF = SLOTS // 2
BUCKET = 16
N_DP = 64
NY = N_DP // (NX * NC)
GROUP = 16 * HEADS
VMEM_LIMIT = 56 * 1024 * 1024


def dp_moves(dy, dx, dc):
    moves = []
    for y in range(NY):
        for x in range(NX):
            for c in range(NC):
                source = (y * NX + x) * NC + c
                target = ((y + dy) % NY * NX + (x + dx) % NX) * NC + (c + dc) % NC
                moves.append((source, target))
    return moves


X_UP, X_DOWN = dp_moves(0, 1, 0), dp_moves(0, -1, 0)
Y_UP, Y_DOWN = dp_moves(1, 0, 0), dp_moves(-1, 0, 0)
SIBLING = dp_moves(0, 0, 1)


def move(array, moves):
    return lax.ppermute(array, "dp", moves)


def pack_kernel(lengths, shifts, own, first, second, out, first_rows, second_rows):
    for rows, state in ((first_rows, first), (second_rows, second)):
        for head in range(HEADS):
            rows[pl.ds(head, ROWS, stride=HEADS), :] = state[:, head * HS : (head + 1) * HS]
        rows[SLOTS : SLOTS + BUCKET, :] = jnp.zeros((BUCKET, HS), jnp.float32)
    me = own[0]

    def piece(j, start):
        target = (me + shifts[j]) & (N_DP - 1)
        out[target, :, 0:HS] = first_rows[pl.ds(start, BUCKET), :].astype(jnp.bfloat16)
        out[target, :, HS : 2 * HS] = second_rows[pl.ds(start, BUCKET), :].astype(jnp.bfloat16)
        return start + lengths[j]

    lax.fori_loop(0, N_DP, piece, jnp.int32(0))


def unpack_kernel(lengths, shifts, own, received, first, second, first_rows, second_rows):
    me = own[0]

    def piece(j, start):
        source = (me - shifts[j]) & (N_DP - 1)
        first_rows[pl.ds(start, BUCKET), :] = received[source, :, 0:HS].astype(jnp.float32)
        second_rows[pl.ds(start, BUCKET), :] = received[source, :, HS : 2 * HS].astype(jnp.float32)
        return start + lengths[j]

    lax.fori_loop(0, N_DP, piece, jnp.int32(0))
    for rows, state in ((first_rows, first), (second_rows, second)):
        for head in range(HEADS):
            state[:, head * HS : (head + 1) * HS] = rows[pl.ds(head, ROWS, stride=HEADS), :]


def weights_kernel(spans, lengths, shifts, own, *refs):
    n = len(spans)
    arrays, (weights, master), (blocks, rows, starts, firsts, places, sems) = refs[:n], refs[n : n + 2], refs[n + 2 :]
    group = pl.program_id(0)
    me = own[0]

    def copy(i):
        half, at, count = spans[i]
        return pltpu.make_async_copy(
            arrays[i], blocks.at[pl.ds(at, count), pl.ds(half * HALF, HALF), :], sems.at[i]
        )

    @pl.when(group == 0)
    def _():
        for i in range(n):
            copy(i).start()

        def piece(j, start):
            starts[j] = start
            firsts[(start + 15) >> 4] = j
            return start + lengths[j]

        lax.fori_loop(0, N_DP, piece, jnp.int32(0))
        my_y, my_x, my_c = me // (NX * NC), (me // NC) % NX, me % NC

        def place(q, carry):
            y = (q // (NX * NC) - my_y) & (NY - 1)
            x = ((q // NC) % NX - my_x) & (NX - 1)
            c = (q - my_c) & (NC - 1)
            y = jnp.where(y < NY // 2, 2 * y, 2 * NY - 1 - 2 * y)
            x = jnp.where(x < NX // 2, 2 * x, 2 * NX - 1 - 2 * x)
            for again in range(2):
                places[again * N_DP + q] = c * (NX * NY) + y * NX + x
                places[(2 + again) * N_DP + q] = c * (NX * NY) + x * NY + y
            return carry

        lax.fori_loop(0, N_DP, place, jnp.int32(0))

    for half in range(2):

        @pl.when(group == half * (HALF // GROUP))
        def _():
            for i in range(n):
                if spans[i][0] == half:
                    copy(i).wait()

    table = jnp.where(group >= HALF // GROUP, 2 * N_DP, 0)
    sublane = lax.broadcasted_iota(jnp.int32, (16, HS), 0)

    def tile(t, carry):
        whole = group * HEADS + t
        offset = pl.multiple_of(whole * 16, 16)
        begin, end = firsts[whole], firsts[whole + 1]

        def chunk(part, carry):
            def load(j):
                base = table + N_DP - shifts[j] + part * 8
                return [blocks[places[base + i], pl.ds(offset, 16), :].astype(jnp.float32) for i in range(8)]

            def later(j, held):
                keep = sublane >= starts[j] - offset
                return [jnp.where(keep, new, old) for new, old in zip(load(j), held)]

            held = lax.fori_loop(begin + 1, end + 1, later, load(begin))
            for i in range(8):
                rows[part * 8 + i, pl.ds(pl.multiple_of(t * 16, 16), 16), :] = held[i]
            return carry

        return lax.fori_loop(0, N_DP // 8, chunk, carry)

    lax.fori_loop(0, HEADS, tile, jnp.int32(0))

    def spread(p, carry):
        for head in range(HEADS):
            weights[p, :, head * HS : (head + 1) * HS] = rows[p, pl.ds(head, 16, stride=HEADS), :].astype(
                jnp.bfloat16
            )
        return carry

    lax.fori_loop(0, N_DP, spread, jnp.int32(0))
    for head in range(HEADS):
        master[:, head * HS : (head + 1) * HS] = rows[me, pl.ds(head, 16, stride=HEADS), :]


def product_kernel(tokens, weights, query, key, total):
    step = pl.program_id(0)
    part = jnp.dot(tokens[...], weights[...], preferred_element_type=jnp.float32)

    @pl.when(step == 0)
    def _():
        total[...] = part

    @pl.when(step > 0)
    def _():
        total[...] += part

    @pl.when(step == pl.num_programs(0) - 1)
    def _():
        query[...] = total[:, : query.shape[1]].astype(query.dtype)
        key[...] = total[:, query.shape[1] :].astype(key.dtype)


SMEM = pl.BlockSpec(memory_space=pltpu.SMEM)
VMEM = pl.BlockSpec(memory_space=pltpu.VMEM)


def gather_weights(master):
    low, high = master[:HALF][None], master[HALF:][None]
    spans, arrays = [], []

    def add(half, at, array):
        spans.append((half, at, array.shape[0]))
        arrays.append(array)

    up = move(low, X_UP)
    down = move(low, X_DOWN)
    row = jnp.concatenate([low, up, down, move(up, X_UP)], axis=0)
    ups, downs = [high], [high]
    for _ in range(3):
        ups.append(move(ups[-1], Y_UP))
        downs.append(move(downs[-1], Y_DOWN))
    column = [high]
    for k in range(1, 4):
        column += [ups[k], downs[k]]
    column = jnp.concatenate(column + [move(ups[3], Y_UP)], axis=0)

    row_ups, row_downs = [row], [row]
    for _ in range(3):
        row_ups.append(move(row_ups[-1], Y_UP))
        row_downs.append(move(row_downs[-1], Y_DOWN))
    last = [move(row_ups[3][: NX // 2], Y_UP), move(row_downs[3][NX // 2 :], Y_DOWN)]
    parts = [row]
    for k in range(1, 4):
        parts += [row_ups[k], row_downs[k]]
    parts += last
    at = 0
    for part in parts:
        add(0, at, part)
        at += part.shape[0]
    add(0, NX * NY, move(jnp.concatenate(parts[:3], axis=0), SIBLING))
    add(0, NX * NY + 3 * NX, move(jnp.concatenate(parts[3:], axis=0), SIBLING))

    column_up = move(column, X_UP)
    column_down = move(column, X_DOWN)
    last = [move(column_up[: NY // 2], X_UP), move(column_down[NY // 2 :], X_DOWN)]
    parts = [column, column_up, column_down] + last
    at = 0
    for part in parts:
        add(1, at, part)
        at += part.shape[0]
    add(1, NX * NY, move(column, SIBLING))
    add(1, NX * NY + NY, move(jnp.concatenate(parts[1:3], axis=0), SIBLING))
    add(1, NX * NY + 3 * NY, move(jnp.concatenate(parts[3:], axis=0), SIBLING))
    return tuple(spans), arrays


def per_device(tokens, old_master, old_first, old_second, piece_lengths, piece_shifts):
    own = lax.axis_index("dp").astype(jnp.int32)[None]
    depth_dev, block_cols = old_master.shape
    state = jax.ShapeDtypeStruct((depth_dev, block_cols), jnp.float32)
    slots = pltpu.VMEM((SLOTS + BUCKET, HS), jnp.float32)
    params = pltpu.CompilerParams(vmem_limit_bytes=VMEM_LIMIT)

    whole_tokens = lax.all_gather(tokens, "tensor", axis=1, tiled=True)

    spans, arrays = gather_weights(old_master.astype(jnp.bfloat16).reshape(SLOTS, HS))

    packed = pl.pallas_call(
        pack_kernel,
        out_shape=jax.ShapeDtypeStruct((N_DP, BUCKET, 2 * HS), jnp.bfloat16),
        in_specs=[SMEM] * 3 + [VMEM] * 2,
        out_specs=VMEM,
        scratch_shapes=[slots, slots],
        name="pack",
    )(piece_lengths, piece_shifts, own, old_first, old_second)
    received = lax.all_to_all(packed, "dp", split_axis=0, concat_axis=0, tiled=True)
    new_first, new_second = pl.pallas_call(
        unpack_kernel,
        out_shape=[state, state],
        in_specs=[SMEM] * 3 + [VMEM],
        out_specs=[VMEM] * 2,
        scratch_shapes=[slots, slots],
        name="unpack",
    )(piece_lengths, piece_shifts, own, received)

    weights, new_master = pl.pallas_call(
        functools.partial(weights_kernel, spans),
        grid=(SLOTS // GROUP,),
        out_shape=[jax.ShapeDtypeStruct((N_DP, depth_dev, block_cols), jnp.bfloat16), state],
        in_specs=[SMEM] * 3 + [pl.BlockSpec(memory_space=pl.ANY)] * len(arrays),
        out_specs=[
            pl.BlockSpec((N_DP, 16, block_cols), lambda g: (0, g, 0)),
            pl.BlockSpec((16, block_cols), lambda g: (g, 0)),
        ],
        scratch_shapes=[
            pltpu.VMEM((N_DP, SLOTS, HS), jnp.bfloat16),
            pltpu.VMEM((N_DP, GROUP, HS), jnp.float32),
            pltpu.SMEM((N_DP,), jnp.int32),
            pltpu.SMEM((SLOTS // 16 + 8,), jnp.int32),
            pltpu.SMEM((4 * N_DP,), jnp.int32),
            pltpu.SemaphoreType.DMA((len(arrays),)),
        ],
        compiler_params=params,
        name="weights",
    )(piece_lengths, piece_shifts, own, *arrays)

    tokens_dev, width = whole_tokens.shape
    query_cols = HQ // lax.axis_size("tensor") * HS
    step = width // 8
    query, key = pl.pallas_call(
        product_kernel,
        grid=(width // step,),
        out_shape=[
            jax.ShapeDtypeStruct((tokens_dev, query_cols), jnp.bfloat16),
            jax.ShapeDtypeStruct((tokens_dev, block_cols - query_cols), jnp.bfloat16),
        ],
        in_specs=[
            pl.BlockSpec((tokens_dev, step), lambda k: (0, k)),
            pl.BlockSpec((step, block_cols), lambda k: (k, 0)),
        ],
        out_specs=[
            pl.BlockSpec((tokens_dev, query_cols), lambda k: (0, 0)),
            pl.BlockSpec((tokens_dev, block_cols - query_cols), lambda k: (0, 0)),
        ],
        scratch_shapes=[pltpu.VMEM((tokens_dev, block_cols), jnp.float32)],
        compiler_params=params,
        cost_estimate=pl.CostEstimate(
            flops=2 * tokens_dev * width * block_cols, bytes_accessed=2 * width * (tokens_dev + block_cols), transcendentals=0
        ),
        name="product",
    )(whole_tokens, weights.reshape(width, block_cols))
    return (new_master, new_first, new_second, query, key)


def solution(mesh):
    blocked = P("dp", "tensor")
    return jax.shard_map(
        per_device,
        mesh=mesh,
        in_specs=(blocked,) * 4 + (P(), P()),
        out_specs=(blocked,) * 5,
        check_vma=False,
    )
```

```python
import functools

import jax
import jax.numpy as jnp
from jax import lax
from jax.experimental import pallas as pl
from jax.experimental.pallas import tpu as pltpu
from jax.sharding import PartitionSpec as P

HQ = 48
HS = 128
NX = 4
NC = 2
HEADS = 7
ROWS = 96
SLOTS = ROWS * HEADS
HALF = SLOTS // 2
BUCKET = 16
N_DP = 64
NY = N_DP // (NX * NC)
GROUP = 16 * HEADS
CHUNK = 32
N_Z = 8
P_LOW = N_DP // N_Z
VMEM_LIMIT = 56 * 1024 * 1024


def dp_index(y, x, c):
    return (y * NX + x) * NC + c


X_GROUPS = [[dp_index(y, x, c) for x in range(NX)] for y in range(NY) for c in range(NC)]
Y_GROUPS = [[dp_index(y, x, c) for y in range(NY) for c in range(NC)] for x in range(NX)]


def pack_kernel(lengths, shifts, own, first, second, out, first_rows, second_rows):
    for rows, state in ((first_rows, first), (second_rows, second)):
        for head in range(HEADS):
            rows[pl.ds(head, ROWS, stride=HEADS), :] = state[:, head * HS : (head + 1) * HS]
        rows[SLOTS : SLOTS + BUCKET, :] = jnp.zeros((BUCKET, HS), jnp.float32)
    me = own[0]

    def piece(j, start):
        target = (me + shifts[j]) & (N_DP - 1)
        out[target, :, 0:HS] = first_rows[pl.ds(start, BUCKET), :].astype(jnp.bfloat16)
        out[target, :, HS : 2 * HS] = second_rows[pl.ds(start, BUCKET), :].astype(jnp.bfloat16)
        return start + lengths[j]

    lax.fori_loop(0, N_DP, piece, jnp.int32(0))


def unpack_kernel(lengths, shifts, own, received, first, second, first_rows, second_rows):
    me = own[0]

    def piece(j, start):
        source = (me - shifts[j]) & (N_DP - 1)
        first_rows[pl.ds(start, BUCKET), :] = received[source, :, 0:HS].astype(jnp.float32)
        second_rows[pl.ds(start, BUCKET), :] = received[source, :, HS : 2 * HS].astype(jnp.float32)
        return start + lengths[j]

    lax.fori_loop(0, N_DP, piece, jnp.int32(0))
    for rows, state in ((first_rows, first), (second_rows, second)):
        for head in range(HEADS):
            state[:, head * HS : (head + 1) * HS] = rows[pl.ds(head, ROWS, stride=HEADS), :]


def product_kernel(places, lengths, shifts, own, gathered, *refs):
    tokens, (master, query, key), (held, rows, weights, total, starts, firsts, sems) = refs[:-10], refs[-10:-7], refs[-7:]
    group = pl.program_id(0)
    me, my_z = own[0], own[1]
    blocks = held.reshape(2 * N_DP, SLOTS, HS)

    def copies(g):
        slots = pl.ds(pl.multiple_of(g * GROUP, GROUP), GROUP)
        return [
            pltpu.make_async_copy(
                gathered.at[:, c, x, slots, :],
                held.at[pl.ds(again * NY, NY), x, c, slots, :],
                sems.at[g, (again * NX + x) * NC + c],
            )
            for again in range(2)
            for x in range(NX)
            for c in range(NC)
        ]

    @pl.when(group == 0)
    def _():
        for g in range(SLOTS // GROUP):
            for copy in copies(g):
                copy.start()

        def piece(j, start):
            starts[j] = start
            firsts[(start + 15) >> 4] = j
            return start + lengths[j]

        lax.fori_loop(0, N_DP, piece, jnp.int32(0))

    for copy in copies(group):
        copy.wait()

    sublane = lax.broadcasted_iota(jnp.int32, (16, HS), 0).astype(jnp.int16)

    def tile(t, carry):
        whole = group * HEADS + t
        offset = pl.multiple_of(whole * 16, 16)
        begin, end = firsts[whole], firsts[whole + 1]

        def chunk(part, carry):
            def load(j):
                base = N_DP - shifts[j] + part * CHUNK
                return [blocks[base + i, pl.ds(offset, 16), :] for i in range(CHUNK)]

            def later(j, kept):
                take = sublane >= (starts[j] - offset).astype(jnp.int16)
                return [jnp.where(take, new, old) for new, old in zip(load(j), kept)]

            kept = lax.fori_loop(begin + 1, end + 1, later, load(begin))
            for i in range(CHUNK):
                rows[part * CHUNK + i, pl.ds(pl.multiple_of(t * 16, 16), 16), :] = kept[i].astype(jnp.float32)
            return carry

        return lax.fori_loop(0, N_DP // CHUNK, chunk, carry)

    lax.fori_loop(0, HEADS, tile, jnp.int32(0))

    def spread(low, carry):
        for i, distance in enumerate(places):
            p = ((my_z + distance) & (N_Z - 1)) * P_LOW + low
            at = pl.ds(pl.multiple_of((i * P_LOW + low) * 16, 16), 16)
            for head in range(HEADS):
                weights[at, head * HS : (head + 1) * HS] = rows[p, pl.ds(head, 16, stride=HEADS), :].astype(
                    jnp.bfloat16
                )
        return carry

    lax.fori_loop(0, P_LOW, spread, jnp.int32(0))
    for head in range(HEADS):
        master[:, head * HS : (head + 1) * HS] = rows[me, pl.ds(head, 16, stride=HEADS), :]

    last = jnp.concatenate([tokens[-2][...], tokens[-1][...]], axis=0)
    columns = jnp.concatenate([block[...] for block in tokens[:-2]] + [last], axis=1)
    part = jnp.dot(columns, weights[...], preferred_element_type=jnp.float32)

    @pl.when(group == 0)
    def _():
        total[...] = part

    @pl.when(group > 0)
    def _():
        total[...] += part

    @pl.when(group == pl.num_programs(0) - 1)
    def _():
        query[...] = total[:, : query.shape[1]].astype(query.dtype)
        key[...] = total[:, query.shape[1] :].astype(key.dtype)


SMEM = pl.BlockSpec(memory_space=pltpu.SMEM)
VMEM = pl.BlockSpec(memory_space=pltpu.VMEM)


def gather_tokens(tokens):
    up = [(z, (z + 1) % N_Z) for z in range(N_Z)]
    down = [(z, (z - 1) % N_Z) for z in range(N_Z)]
    half = tokens.shape[0] // 2
    from_below, from_above = tokens, tokens
    distances, arrays = [0], [tokens]
    for distance in range(1, N_Z // 2):
        from_below = lax.ppermute(from_below, "tensor", up)
        from_above = lax.ppermute(from_above, "tensor", down)
        distances += [-distance, distance]
        arrays += [from_below, from_above]
    distances.append(N_Z // 2)
    arrays.append(lax.ppermute(from_below[:half], "tensor", up))
    arrays.append(lax.ppermute(from_above[half:], "tensor", down))
    return tuple(distances), arrays


def per_device(tokens, old_master, old_first, old_second, piece_lengths, piece_shifts):
    own = jnp.stack([lax.axis_index("dp"), lax.axis_index("tensor")]).astype(jnp.int32)
    depth_dev, block_cols = old_master.shape
    state = jax.ShapeDtypeStruct((depth_dev, block_cols), jnp.float32)
    slots = pltpu.VMEM((SLOTS + BUCKET, HS), jnp.float32)

    column = old_master.astype(jnp.bfloat16).reshape(SLOTS, HS)
    row = lax.all_gather(column, "dp", axis_index_groups=X_GROUPS, axis=0, tiled=True)
    gathered = lax.all_gather(row, "dp", axis_index_groups=Y_GROUPS, axis=0, tiled=True)
    gathered = gathered.reshape(NY, NC, NX, SLOTS, HS)

    tokens_dev, width = tokens.shape
    old = jnp.arange(width, dtype=jnp.int32)
    low, depth = old // depth_dev, old % depth_dev
    new = (depth // 16 * P_LOW + low) * 16 + depth % 16
    order = (new[:, None] == old[None, :]).astype(jnp.bfloat16)
    ordered = jnp.dot(tokens, order, preferred_element_type=jnp.float32).astype(jnp.bfloat16)
    distances, blocks = gather_tokens(ordered)

    packed = pl.pallas_call(
        pack_kernel,
        out_shape=jax.ShapeDtypeStruct((N_DP, BUCKET, 2 * HS), jnp.bfloat16),
        in_specs=[SMEM] * 3 + [VMEM] * 2,
        out_specs=VMEM,
        scratch_shapes=[slots, slots],
        name="pack",
    )(piece_lengths, piece_shifts, own, old_first, old_second)
    received = lax.all_to_all(packed, "dp", split_axis=0, concat_axis=0, tiled=True)
    new_first, new_second = pl.pallas_call(
        unpack_kernel,
        out_shape=[state, state],
        in_specs=[SMEM] * 3 + [VMEM],
        out_specs=[VMEM] * 2,
        scratch_shapes=[slots, slots],
        name="unpack",
    )(piece_lengths, piece_shifts, own, received)

    query_cols = HQ // lax.axis_size("tensor") * HS
    key_cols = block_cols - query_cols
    group_cols = P_LOW * 16
    new_master, query, key = pl.pallas_call(
        functools.partial(product_kernel, distances),
        grid=(SLOTS // GROUP,),
        out_shape=[
            state,
            jax.ShapeDtypeStruct((tokens_dev, query_cols), jnp.bfloat16),
            jax.ShapeDtypeStruct((tokens_dev, key_cols), jnp.bfloat16),
        ],
        in_specs=[SMEM] * 3
        + [pl.BlockSpec(memory_space=pl.ANY)]
        + [pl.BlockSpec((block.shape[0], group_cols), lambda g: (0, g)) for block in blocks],
        out_specs=[
            pl.BlockSpec((16, block_cols), lambda g: (g, 0)),
            pl.BlockSpec((tokens_dev, query_cols), lambda g: (0, 0)),
            pl.BlockSpec((tokens_dev, key_cols), lambda g: (0, 0)),
        ],
        scratch_shapes=[
            pltpu.VMEM((2 * NY, NX, NC, SLOTS, HS), jnp.bfloat16),
            pltpu.VMEM((N_DP, GROUP, HS), jnp.float32),
            pltpu.VMEM((N_Z * group_cols, block_cols), jnp.bfloat16),
            pltpu.VMEM((tokens_dev, block_cols), jnp.float32),
            pltpu.SMEM((N_DP,), jnp.int32),
            pltpu.SMEM((SLOTS // 16 + 8,), jnp.int32),
            pltpu.SemaphoreType.DMA((SLOTS // GROUP, 2 * NX * NC)),
        ],
        compiler_params=pltpu.CompilerParams(vmem_limit_bytes=VMEM_LIMIT),
        cost_estimate=pl.CostEstimate(
            flops=2 * tokens_dev * width * N_Z * block_cols,
            bytes_accessed=2 * width * N_Z * (tokens_dev + block_cols),
            transcendentals=0,
        ),
        name="product",
    )(piece_lengths, piece_shifts, own, gathered, *blocks)
    return (new_master, new_first, new_second, query, key)


def solution(mesh):
    blocked = P("dp", "tensor")
    return jax.shard_map(
        per_device,
        mesh=mesh,
        in_specs=(blocked,) * 4 + (P(), P()),
        out_specs=(blocked,) * 5,
        check_vma=False,
    )
```

```python
import functools

import jax
import jax.numpy as jnp
from jax import lax
from jax.experimental import pallas as pl
from jax.experimental.pallas import tpu as pltpu
from jax.sharding import PartitionSpec as P

HQ = 48
HS = 128
HEADS = 7
ROWS = 96
SLOTS = ROWS * HEADS
HALF = SLOTS // 2
BUCKET = 16
N_DP = 64
GROUP_ROWS = 32
GROUP = GROUP_ROWS * HEADS
CHUNK = 32
N_Z = 8
P_LOW = N_DP // N_Z
VMEM_LIMIT = 56 * 1024 * 1024


def pack_kernel(lengths, shifts, own, first, second, out, first_rows, second_rows):
    for rows, state in ((first_rows, first), (second_rows, second)):
        for head in range(HEADS):
            rows[pl.ds(head, ROWS, stride=HEADS), :] = state[:, head * HS : (head + 1) * HS]
        rows[SLOTS : SLOTS + BUCKET, :] = jnp.zeros((BUCKET, HS), jnp.float32)
    me = own[0]

    def piece(j, start):
        target = (me + shifts[j]) & (N_DP - 1)
        out[target, :, 0:HS] = first_rows[pl.ds(start, BUCKET), :].astype(jnp.bfloat16)
        out[target, :, HS : 2 * HS] = second_rows[pl.ds(start, BUCKET), :].astype(jnp.bfloat16)
        return start + lengths[j]

    lax.fori_loop(0, N_DP, piece, jnp.int32(0))


def unpack_kernel(lengths, shifts, own, received, first, second, first_rows, second_rows):
    me = own[0]

    def piece(j, start):
        source = (me - shifts[j]) & (N_DP - 1)
        first_rows[pl.ds(start, BUCKET), :] = received[source, :, 0:HS].astype(jnp.float32)
        second_rows[pl.ds(start, BUCKET), :] = received[source, :, HS : 2 * HS].astype(jnp.float32)
        return start + lengths[j]

    lax.fori_loop(0, N_DP, piece, jnp.int32(0))
    for rows, state in ((first_rows, first), (second_rows, second)):
        for head in range(HEADS):
            state[:, head * HS : (head + 1) * HS] = rows[pl.ds(head, ROWS, stride=HEADS), :]


def product_kernel(places, lengths, shifts, own, gathered, *refs):
    tokens, (master, query, key), (blocks, rows, weights, total, starts, firsts, sems) = refs[:-10], refs[-10:-7], refs[-7:]
    group = pl.program_id(0)
    me, my_z = own[0], own[1]
    def copies(g):
        slots = pl.ds(pl.multiple_of(g * GROUP, GROUP), GROUP)
        return [
            pltpu.make_async_copy(
                gathered.at[:, slots, :], blocks.at[pl.ds(again * N_DP, N_DP), slots, :], sems.at[g, again]
            )
            for again in range(2)
        ]

    @pl.when(group == 0)
    def _():
        for g in range(SLOTS // GROUP):
            for copy in copies(g):
                copy.start()

        def piece(j, start):
            starts[j] = start
            firsts[(start + 15) >> 4] = j
            return start + lengths[j]

        lax.fori_loop(0, N_DP, piece, jnp.int32(0))

    for copy in copies(group):
        copy.wait()

    sublane = lax.broadcasted_iota(jnp.int32, (16, HS), 0).astype(jnp.int16)

    def tile(t, carry):
        whole = group * (GROUP // 16) + t
        offset = pl.multiple_of(whole * 16, 16)
        begin, end = firsts[whole], firsts[whole + 1]

        def chunk(part, carry):
            def load(j):
                base = N_DP - shifts[j] + part * CHUNK
                return [blocks[base + i, pl.ds(offset, 16), :] for i in range(CHUNK)]

            def later(j, kept):
                take = sublane >= (starts[j] - offset).astype(jnp.int16)
                return [jnp.where(take, new, old) for new, old in zip(load(j), kept)]

            kept = lax.fori_loop(begin + 1, end + 1, later, load(begin))
            for i in range(CHUNK):
                rows[part * CHUNK + i, pl.ds(pl.multiple_of(t * 16, 16), 16), :] = kept[i].astype(jnp.float32)
            return carry

        return lax.fori_loop(0, N_DP // CHUNK, chunk, carry)

    lax.fori_loop(0, GROUP // 16, tile, jnp.int32(0))

    def spread(low, carry):
        for i, distance in enumerate(places):
            p = ((my_z + distance) & (N_Z - 1)) * P_LOW + low
            at = pl.ds(pl.multiple_of((i * P_LOW + low) * GROUP_ROWS, GROUP_ROWS), GROUP_ROWS)
            for head in range(HEADS):
                weights[at, head * HS : (head + 1) * HS] = rows[p, pl.ds(head, GROUP_ROWS, stride=HEADS), :].astype(
                    jnp.bfloat16
                )
        return carry

    lax.fori_loop(0, P_LOW, spread, jnp.int32(0))
    for head in range(HEADS):
        master[:, head * HS : (head + 1) * HS] = rows[me, pl.ds(head, GROUP_ROWS, stride=HEADS), :]

    last = jnp.concatenate([tokens[-2][...], tokens[-1][...]], axis=0)
    columns = jnp.concatenate([block[...] for block in tokens[:-2]] + [last], axis=1)
    part = jnp.dot(columns, weights[...], preferred_element_type=jnp.float32)

    @pl.when(group == 0)
    def _():
        total[...] = part

    @pl.when(group > 0)
    def _():
        total[...] += part

    @pl.when(group == pl.num_programs(0) - 1)
    def _():
        query[...] = total[:, : query.shape[1]].astype(query.dtype)
        key[...] = total[:, query.shape[1] :].astype(key.dtype)


SMEM = pl.BlockSpec(memory_space=pltpu.SMEM)
VMEM = pl.BlockSpec(memory_space=pltpu.VMEM)


def gather_tokens(tokens):
    up = [(z, (z + 1) % N_Z) for z in range(N_Z)]
    down = [(z, (z - 1) % N_Z) for z in range(N_Z)]
    half = tokens.shape[0] // 2
    from_below, from_above = tokens, tokens
    distances, arrays = [0], [tokens]
    for distance in range(1, N_Z // 2):
        from_below = lax.ppermute(from_below, "tensor", up)
        from_above = lax.ppermute(from_above, "tensor", down)
        distances += [-distance, distance]
        arrays += [from_below, from_above]
    distances.append(N_Z // 2)
    arrays.append(lax.ppermute(from_below[:half], "tensor", up))
    arrays.append(lax.ppermute(from_above[half:], "tensor", down))
    return tuple(distances), arrays


def per_device(tokens, old_master, old_first, old_second, piece_lengths, piece_shifts):
    own = jnp.stack([lax.axis_index("dp"), lax.axis_index("tensor")]).astype(jnp.int32)
    depth_dev, block_cols = old_master.shape
    state = jax.ShapeDtypeStruct((depth_dev, block_cols), jnp.float32)
    slots = pltpu.VMEM((SLOTS + BUCKET, HS), jnp.float32)

    column = old_master.astype(jnp.bfloat16).reshape(SLOTS, HS)
    gathered = lax.all_gather(column, "dp")

    tokens_dev, width = tokens.shape
    old = jnp.arange(width, dtype=jnp.int32)
    low, depth = old // depth_dev, old % depth_dev
    new = (depth // GROUP_ROWS * P_LOW + low) * GROUP_ROWS + depth % GROUP_ROWS
    order = (new[:, None] == old[None, :]).astype(jnp.bfloat16)
    ordered = jnp.dot(tokens, order, preferred_element_type=jnp.float32).astype(jnp.bfloat16)
    distances, blocks = gather_tokens(ordered)

    packed = pl.pallas_call(
        pack_kernel,
        out_shape=jax.ShapeDtypeStruct((N_DP, BUCKET, 2 * HS), jnp.bfloat16),
        in_specs=[SMEM] * 3 + [VMEM] * 2,
        out_specs=VMEM,
        scratch_shapes=[slots, slots],
        name="pack",
    )(piece_lengths, piece_shifts, own, old_first, old_second)
    received = lax.all_to_all(packed, "dp", split_axis=0, concat_axis=0, tiled=True)
    new_first, new_second = pl.pallas_call(
        unpack_kernel,
        out_shape=[state, state],
        in_specs=[SMEM] * 3 + [VMEM],
        out_specs=[VMEM] * 2,
        scratch_shapes=[slots, slots],
        name="unpack",
    )(piece_lengths, piece_shifts, own, received)

    query_cols = HQ // lax.axis_size("tensor") * HS
    key_cols = block_cols - query_cols
    group_cols = P_LOW * GROUP_ROWS
    new_master, query, key = pl.pallas_call(
        functools.partial(product_kernel, distances),
        grid=(SLOTS // GROUP,),
        out_shape=[
            state,
            jax.ShapeDtypeStruct((tokens_dev, query_cols), jnp.bfloat16),
            jax.ShapeDtypeStruct((tokens_dev, key_cols), jnp.bfloat16),
        ],
        in_specs=[SMEM] * 3
        + [pl.BlockSpec(memory_space=pl.ANY)]
        + [pl.BlockSpec((block.shape[0], group_cols), lambda g: (0, g)) for block in blocks],
        out_specs=[
            pl.BlockSpec((GROUP_ROWS, block_cols), lambda g: (g, 0)),
            pl.BlockSpec((tokens_dev, query_cols), lambda g: (0, 0)),
            pl.BlockSpec((tokens_dev, key_cols), lambda g: (0, 0)),
        ],
        scratch_shapes=[
            pltpu.VMEM((2 * N_DP, SLOTS, HS), jnp.bfloat16),
            pltpu.VMEM((N_DP, GROUP, HS), jnp.float32),
            pltpu.VMEM((N_Z * group_cols, block_cols), jnp.bfloat16),
            pltpu.VMEM((tokens_dev, block_cols), jnp.float32),
            pltpu.SMEM((N_DP,), jnp.int32),
            pltpu.SMEM((SLOTS // 16 + 8,), jnp.int32),
            pltpu.SemaphoreType.DMA((SLOTS // GROUP, 2)),
        ],
        compiler_params=pltpu.CompilerParams(vmem_limit_bytes=VMEM_LIMIT),
        cost_estimate=pl.CostEstimate(
            flops=2 * tokens_dev * width * N_Z * block_cols,
            bytes_accessed=2 * width * N_Z * (tokens_dev + block_cols),
            transcendentals=0,
        ),
        name="product",
    )(piece_lengths, piece_shifts, own, gathered, *blocks)
    return (new_master, new_first, new_second, query, key)


def solution(mesh):
    blocked = P("dp", "tensor")
    return jax.shard_map(
        per_device,
        mesh=mesh,
        in_specs=(blocked,) * 4 + (P(), P()),
        out_specs=(blocked,) * 5,
        check_vma=False,
    )
```

```python
import functools

import jax
import jax.numpy as jnp
from jax import lax
from jax.experimental import pallas as pl
from jax.experimental.pallas import tpu as pltpu
from jax.sharding import PartitionSpec as P

HQ = 48
HS = 128
NX = 4
NC = 2
HEADS = 7
ROWS = 96
SLOTS = ROWS * HEADS
HALF = SLOTS // 2
BUCKET = 16
N_DP = 64
NY = N_DP // (NX * NC)
GROUP_ROWS = 32
GROUP = GROUP_ROWS * HEADS
GROUPS = SLOTS // GROUP
CHUNK = 32
N_Z = 8
P_LOW = N_DP // N_Z
VMEM_LIMIT = 56 * 1024 * 1024


def dp_index(y, x, c):
    return (y * NX + x) * NC + c


X_GROUPS = [[dp_index(y, x, c) for x in range(NX)] for y in range(NY) for c in range(NC)]
Y_GROUPS = [[dp_index(y, x, c) for y in range(NY) for c in range(NC)] for x in range(NX)]


def pack_kernel(lengths, shifts, own, first, second, after, out, first_rows, second_rows):
    for rows, state in ((first_rows, first), (second_rows, second)):
        for head in range(HEADS):
            rows[pl.ds(head, ROWS, stride=HEADS), :] = state[:, head * HS : (head + 1) * HS]
        rows[SLOTS : SLOTS + BUCKET, :] = jnp.zeros((BUCKET, HS), jnp.float32)
    me = own[0]

    def piece(j, start):
        target = (me + shifts[j]) & (N_DP - 1)
        out[target, :, 0:HS] = first_rows[pl.ds(start, BUCKET), :].astype(jnp.bfloat16)
        out[target, :, HS : 2 * HS] = second_rows[pl.ds(start, BUCKET), :].astype(jnp.bfloat16)
        return start + lengths[j]

    lax.fori_loop(0, N_DP, piece, jnp.int32(0))


def unpack_kernel(lengths, shifts, own, received, after, first, second, first_rows, second_rows):
    me = own[0]

    def piece(j, start):
        source = (me - shifts[j]) & (N_DP - 1)
        first_rows[pl.ds(start, BUCKET), :] = received[source, :, 0:HS].astype(jnp.float32)
        second_rows[pl.ds(start, BUCKET), :] = received[source, :, HS : 2 * HS].astype(jnp.float32)
        return start + lengths[j]

    lax.fori_loop(0, N_DP, piece, jnp.int32(0))
    for rows, state in ((first_rows, first), (second_rows, second)):
        for head in range(HEADS):
            state[:, head * HS : (head + 1) * HS] = rows[pl.ds(head, ROWS, stride=HEADS), :]


def product_kernel(places, lengths, shifts, own, gathered, *refs):
    tokens, (master, query, key), (held, rows, weights, total, starts, firsts, sems) = refs[:-10], refs[-10:-7], refs[-7:]
    group = pl.program_id(0)
    me, my_z = own[0], own[1]
    blocks = held.reshape(2 * N_DP, SLOTS, HS)

    def copies(g):
        slots = pl.ds(pl.multiple_of(g * GROUP, GROUP), GROUP)
        return [
            pltpu.make_async_copy(
                gathered.at[:, c, x, slots, :],
                held.at[pl.ds(again * NY, NY), x, c, slots, :],
                sems.at[g, (again * NX + x) * NC + c],
            )
            for again in range(2)
            for x in range(NX)
            for c in range(NC)
        ]

    @pl.when(group == 0)
    def _():
        for g in range(GROUPS):
            for copy in copies(g):
                copy.start()

        def piece(j, start):
            starts[j] = start
            firsts[(start + 15) >> 4] = j
            return start + lengths[j]

        lax.fori_loop(0, N_DP, piece, jnp.int32(0))

    for copy in copies(group):
        copy.wait()

    sublane = lax.broadcasted_iota(jnp.int32, (16, HS), 0).astype(jnp.int16)

    def tile(t, carry):
        whole = group * (GROUP // 16) + t
        offset = pl.multiple_of(whole * 16, 16)
        begin, end = firsts[whole], firsts[whole + 1]

        def chunk(part, carry):
            def load(j):
                base = N_DP - shifts[j] + part * CHUNK
                return [blocks[base + i, pl.ds(offset, 16), :] for i in range(CHUNK)]

            def later(j, kept):
                take = sublane >= (starts[j] - offset).astype(jnp.int16)
                return [jnp.where(take, new, old) for new, old in zip(load(j), kept)]

            kept = lax.fori_loop(begin + 1, end + 1, later, load(begin))
            for i in range(CHUNK):
                rows[part * CHUNK + i, pl.ds(pl.multiple_of(t * 16, 16), 16), :] = kept[i].astype(jnp.float32)
            return carry

        return lax.fori_loop(0, N_DP // CHUNK, chunk, carry)

    lax.fori_loop(0, GROUP // 16, tile, jnp.int32(0))

    def spread(low, carry):
        for i, distance in enumerate(places):
            p = ((my_z + distance) & (N_Z - 1)) * P_LOW + low
            at = pl.ds(pl.multiple_of((i * P_LOW + low) * GROUP_ROWS, GROUP_ROWS), GROUP_ROWS)
            for head in range(HEADS):
                weights[at, head * HS : (head + 1) * HS] = rows[p, pl.ds(head, GROUP_ROWS, stride=HEADS), :].astype(
                    jnp.bfloat16
                )
        return carry

    lax.fori_loop(0, P_LOW, spread, jnp.int32(0))
    for head in range(HEADS):
        master[:, head * HS : (head + 1) * HS] = rows[me, pl.ds(head, GROUP_ROWS, stride=HEADS), :]

    last = jnp.concatenate([tokens[-2][...], tokens[-1][...]], axis=0)
    columns = jnp.concatenate([block[...] for block in tokens[:-2]] + [last], axis=1)
    part = jnp.dot(columns, weights[...], preferred_element_type=jnp.float32)

    @pl.when(group == 0)
    def _():
        total[...] = part

    @pl.when(group > 0)
    def _():
        total[...] += part

    @pl.when(group == pl.num_programs(0) - 1)
    def _():
        query[...] = total[:, : query.shape[1]].astype(query.dtype)
        key[...] = total[:, query.shape[1] :].astype(key.dtype)


SMEM = pl.BlockSpec(memory_space=pltpu.SMEM)
VMEM = pl.BlockSpec(memory_space=pltpu.VMEM)
ANY = pl.BlockSpec(memory_space=pl.ANY)


def gather_tokens(tokens):
    up = [(z, (z + 1) % N_Z) for z in range(N_Z)]
    down = [(z, (z - 1) % N_Z) for z in range(N_Z)]
    half = tokens.shape[0] // 2
    from_below, from_above = tokens, tokens
    distances, arrays = [0], [tokens]
    for distance in range(1, N_Z // 2):
        from_below = lax.ppermute(from_below, "tensor", up)
        from_above = lax.ppermute(from_above, "tensor", down)
        distances += [-distance, distance]
        arrays += [from_below, from_above]
    distances.append(N_Z // 2)
    arrays.append(lax.ppermute(from_below[:half], "tensor", up))
    arrays.append(lax.ppermute(from_above[half:], "tensor", down))
    return tuple(distances), arrays


def per_device(tokens, old_master, old_first, old_second, piece_lengths, piece_shifts):
    own = jnp.stack([lax.axis_index("dp"), lax.axis_index("tensor")]).astype(jnp.int32)
    depth_dev, block_cols = old_master.shape
    state = jax.ShapeDtypeStruct((depth_dev, block_cols), jnp.float32)
    slots = pltpu.VMEM((SLOTS + BUCKET, HS), jnp.float32)

    column = old_master.astype(jnp.bfloat16).reshape(SLOTS, HS)
    row = lax.all_gather(column, "dp", axis_index_groups=X_GROUPS, axis=0, tiled=True)
    gathered = lax.all_gather(row, "dp", axis_index_groups=Y_GROUPS, axis=0, tiled=True)
    gathered = gathered.reshape(NY, NC, NX, SLOTS, HS)

    tokens_dev, width = tokens.shape
    old = jnp.arange(width, dtype=jnp.int32)
    low, depth = old // depth_dev, old % depth_dev
    new = (depth // GROUP_ROWS * P_LOW + low) * GROUP_ROWS + depth % GROUP_ROWS
    order = (new[:, None] == old[None, :]).astype(jnp.bfloat16)
    ordered = jnp.dot(tokens, order, preferred_element_type=jnp.float32).astype(jnp.bfloat16)
    distances, blocks = gather_tokens(ordered)

    packed = pl.pallas_call(
        pack_kernel,
        out_shape=jax.ShapeDtypeStruct((N_DP, BUCKET, 2 * HS), jnp.bfloat16),
        in_specs=[SMEM] * 3 + [VMEM] * 2 + [ANY],
        out_specs=VMEM,
        scratch_shapes=[slots, slots],
        name="pack",
    )(piece_lengths, piece_shifts, own, old_first, old_second, blocks[-1])
    received = lax.all_to_all(packed, "dp", split_axis=0, concat_axis=0, tiled=True)
    query_cols = HQ // lax.axis_size("tensor") * HS
    key_cols = block_cols - query_cols
    group_cols = P_LOW * GROUP_ROWS
    new_master, query, key = pl.pallas_call(
        functools.partial(product_kernel, distances),
        grid=(GROUPS,),
        out_shape=[
            state,
            jax.ShapeDtypeStruct((tokens_dev, query_cols), jnp.bfloat16),
            jax.ShapeDtypeStruct((tokens_dev, key_cols), jnp.bfloat16),
        ],
        in_specs=[SMEM] * 3
        + [pl.BlockSpec(memory_space=pl.ANY)]
        + [pl.BlockSpec((block.shape[0], group_cols), lambda g: (0, g)) for block in blocks],
        out_specs=[
            pl.BlockSpec((GROUP_ROWS, block_cols), lambda g: (g, 0)),
            pl.BlockSpec((tokens_dev, query_cols), lambda g: (0, 0)),
            pl.BlockSpec((tokens_dev, key_cols), lambda g: (0, 0)),
        ],
        scratch_shapes=[
            pltpu.VMEM((2 * NY, NX, NC, SLOTS, HS), jnp.bfloat16),
            pltpu.VMEM((N_DP, GROUP, HS), jnp.float32),
            pltpu.VMEM((N_Z * group_cols, block_cols), jnp.bfloat16),
            pltpu.VMEM((tokens_dev, block_cols), jnp.float32),
            pltpu.SMEM((N_DP,), jnp.int32),
            pltpu.SMEM((SLOTS // 16 + 8,), jnp.int32),
            pltpu.SemaphoreType.DMA((GROUPS, 2 * NX * NC)),
        ],
        compiler_params=pltpu.CompilerParams(vmem_limit_bytes=VMEM_LIMIT),
        cost_estimate=pl.CostEstimate(
            flops=2 * tokens_dev * width * N_Z * block_cols,
            bytes_accessed=2 * width * N_Z * (tokens_dev + block_cols),
            transcendentals=0,
        ),
        name="product",
    )(piece_lengths, piece_shifts, own, gathered, *blocks)
    new_first, new_second = pl.pallas_call(
        unpack_kernel,
        out_shape=[state, state],
        in_specs=[SMEM] * 3 + [VMEM, ANY],
        out_specs=[VMEM] * 2,
        scratch_shapes=[slots, slots],
        name="unpack",
    )(piece_lengths, piece_shifts, own, received, key)

    return (new_master, new_first, new_second, query, key)


def solution(mesh):
    blocked = P("dp", "tensor")
    return jax.shard_map(
        per_device,
        mesh=mesh,
        in_specs=(blocked,) * 4 + (P(), P()),
        out_specs=(blocked,) * 5,
        check_vma=False,
    )
```

```python
import functools

import jax
import jax.numpy as jnp
from jax import lax
from jax.experimental import pallas as pl
from jax.experimental.pallas import tpu as pltpu
from jax.sharding import PartitionSpec as P

HQ = 48
HS = 128
NX = 4
NC = 2
HEADS = 7
ROWS = 96
SLOTS = ROWS * HEADS
HALF = SLOTS // 2
BUCKET = 16
N_DP = 64
NY = N_DP // (NX * NC)
GROUP_ROWS = 32
GROUP = GROUP_ROWS * HEADS
GROUPS = SLOTS // GROUP
CHUNK = 32
N_Z = 8
P_LOW = N_DP // N_Z
VMEM_LIMIT = 56 * 1024 * 1024


def dp_index(y, x, c):
    return (y * NX + x) * NC + c


X_GROUPS = [[dp_index(y, x, c) for x in range(NX)] for y in range(NY) for c in range(NC)]
Y_GROUPS = [[dp_index(y, x, c) for y in range(NY) for c in range(NC)] for x in range(NX)]


def pack_kernel(lengths, shifts, own, first, second, out, first_rows, second_rows):
    for rows, state in ((first_rows, first), (second_rows, second)):
        for head in range(HEADS):
            rows[pl.ds(head, ROWS, stride=HEADS), :] = state[:, head * HS : (head + 1) * HS]
        rows[SLOTS : SLOTS + BUCKET, :] = jnp.zeros((BUCKET, HS), jnp.float32)
    me = own[0]

    def piece(j, start):
        target = (me + shifts[j]) & (N_DP - 1)
        out[target, :, 0:HS] = first_rows[pl.ds(start, BUCKET), :].astype(jnp.bfloat16)
        out[target, :, HS : 2 * HS] = second_rows[pl.ds(start, BUCKET), :].astype(jnp.bfloat16)
        return start + lengths[j]

    lax.fori_loop(0, N_DP, piece, jnp.int32(0))


def unpack_kernel(lengths, shifts, own, received, first, second, first_rows, second_rows):
    me = own[0]

    def piece(j, start):
        source = (me - shifts[j]) & (N_DP - 1)
        first_rows[pl.ds(start, BUCKET), :] = received[source, :, 0:HS].astype(jnp.float32)
        second_rows[pl.ds(start, BUCKET), :] = received[source, :, HS : 2 * HS].astype(jnp.float32)
        return start + lengths[j]

    lax.fori_loop(0, N_DP, piece, jnp.int32(0))
    for rows, state in ((first_rows, first), (second_rows, second)):
        for head in range(HEADS):
            state[:, head * HS : (head + 1) * HS] = rows[pl.ds(head, ROWS, stride=HEADS), :]


def product_kernel(places, lengths, shifts, own, gathered, *refs):
    tokens, (master, query, key), (held, rows, weights, total, starts, firsts, sems) = refs[:-10], refs[-10:-7], refs[-7:]
    group = pl.program_id(0)
    me, my_z = own[0], own[1]
    blocks = held.reshape(2 * N_DP, SLOTS, HS)

    def copies(g):
        slots = pl.ds(pl.multiple_of(g * GROUP, GROUP), GROUP)
        return [
            pltpu.make_async_copy(
                gathered.at[:, c, x, slots, :],
                held.at[pl.ds(again * NY, NY), x, c, slots, :],
                sems.at[g, (again * NX + x) * NC + c],
            )
            for again in range(2)
            for x in range(NX)
            for c in range(NC)
        ]

    @pl.when(group == 0)
    def _():
        for g in range(GROUPS):
            for copy in copies(g):
                copy.start()

        def piece(j, start):
            starts[j] = start
            firsts[(start + 15) >> 4] = j
            return start + lengths[j]

        lax.fori_loop(0, N_DP, piece, jnp.int32(0))

    for copy in copies(group):
        copy.wait()

    sublane = lax.broadcasted_iota(jnp.int32, (16, HS), 0).astype(jnp.int16)

    def tile(t, carry):
        whole = group * (GROUP // 16) + t
        offset = pl.multiple_of(whole * 16, 16)
        begin, end = firsts[whole], firsts[whole + 1]

        def chunk(part, carry):
            def load(j):
                base = N_DP - shifts[j] + part * CHUNK
                return [blocks[base + i, pl.ds(offset, 16), :] for i in range(CHUNK)]

            def later(j, kept):
                take = sublane >= (starts[j] - offset).astype(jnp.int16)
                return [jnp.where(take, new, old) for new, old in zip(load(j), kept)]

            kept = lax.fori_loop(begin + 1, end + 1, later, load(begin))
            for i in range(CHUNK):
                rows[part * CHUNK + i, pl.ds(pl.multiple_of(t * 16, 16), 16), :] = kept[i].astype(jnp.float32)
            return carry

        return lax.fori_loop(0, N_DP // CHUNK, chunk, carry)

    lax.fori_loop(0, GROUP // 16, tile, jnp.int32(0))

    def spread(low, carry):
        for i, distance in enumerate(places):
            p = ((my_z + distance) & (N_Z - 1)) * P_LOW + low
            at = pl.ds(pl.multiple_of((i * P_LOW + low) * GROUP_ROWS, GROUP_ROWS), GROUP_ROWS)
            for head in range(HEADS):
                weights[at, head * HS : (head + 1) * HS] = rows[p, pl.ds(head, GROUP_ROWS, stride=HEADS), :].astype(
                    jnp.bfloat16
                )
        return carry

    lax.fori_loop(0, P_LOW, spread, jnp.int32(0))
    for head in range(HEADS):
        master[:, head * HS : (head + 1) * HS] = rows[me, pl.ds(head, GROUP_ROWS, stride=HEADS), :]

    last = jnp.concatenate([tokens[-2][...], tokens[-1][...]], axis=0)
    columns = jnp.concatenate([block[...] for block in tokens[:-2]] + [last], axis=1)
    part = jnp.dot(columns, weights[...], preferred_element_type=jnp.float32)

    @pl.when(group == 0)
    def _():
        total[...] = part

    @pl.when(group > 0)
    def _():
        total[...] += part

    @pl.when(group == pl.num_programs(0) - 1)
    def _():
        query[...] = total[:, : query.shape[1]].astype(query.dtype)
        key[...] = total[:, query.shape[1] :].astype(key.dtype)


SMEM = pl.BlockSpec(memory_space=pltpu.SMEM)
VMEM = pl.BlockSpec(memory_space=pltpu.VMEM)


def gather_tokens(tokens, moments):
    up = [(z, (z + 1) % N_Z) for z in range(N_Z)]
    down = [(z, (z - 1) % N_Z) for z in range(N_Z)]
    half = tokens.shape[0] // 2
    from_below, from_above = tokens, tokens
    distances, arrays = [0], [tokens]
    for distance in range(1, N_Z // 2):
        from_below = lax.ppermute(from_below, "tensor", up)
        from_above = lax.ppermute(from_above, "tensor", down)
        distances += [-distance, distance]
        if distance == 2:
            from_below, from_above, moments = lax.optimization_barrier((from_below, from_above, moments))
        arrays += [from_below, from_above]
    distances.append(N_Z // 2)
    arrays.append(lax.ppermute(from_below[:half], "tensor", up))
    arrays.append(lax.ppermute(from_above[half:], "tensor", down))
    return tuple(distances), arrays, moments


def per_device(tokens, old_master, old_first, old_second, piece_lengths, piece_shifts):
    own = jnp.stack([lax.axis_index("dp"), lax.axis_index("tensor")]).astype(jnp.int32)
    depth_dev, block_cols = old_master.shape
    state = jax.ShapeDtypeStruct((depth_dev, block_cols), jnp.float32)
    slots = pltpu.VMEM((SLOTS + BUCKET, HS), jnp.float32)

    column = old_master.astype(jnp.bfloat16).reshape(SLOTS, HS)
    row = lax.all_gather(column, "dp", axis_index_groups=X_GROUPS, axis=0, tiled=True)
    gathered = lax.all_gather(row, "dp", axis_index_groups=Y_GROUPS, axis=0, tiled=True)
    gathered = gathered.reshape(NY, NC, NX, SLOTS, HS)

    tokens_dev, width = tokens.shape
    old = jnp.arange(width, dtype=jnp.int32)
    low, depth = old // depth_dev, old % depth_dev
    new = (depth // GROUP_ROWS * P_LOW + low) * GROUP_ROWS + depth % GROUP_ROWS
    order = (new[:, None] == old[None, :]).astype(jnp.bfloat16)
    ordered = jnp.dot(tokens, order, preferred_element_type=jnp.float32).astype(jnp.bfloat16)
    packed = pl.pallas_call(
        pack_kernel,
        out_shape=jax.ShapeDtypeStruct((N_DP, BUCKET, 2 * HS), jnp.bfloat16),
        in_specs=[SMEM] * 3 + [VMEM] * 2,
        out_specs=VMEM,
        scratch_shapes=[slots, slots],
        name="pack",
    )(piece_lengths, piece_shifts, own, old_first, old_second)
    received = lax.all_to_all(packed, "dp", split_axis=0, concat_axis=0, tiled=True)
    new_first, new_second = pl.pallas_call(
        unpack_kernel,
        out_shape=[state, state],
        in_specs=[SMEM] * 3 + [VMEM],
        out_specs=[VMEM] * 2,
        scratch_shapes=[slots, slots],
        name="unpack",
    )(piece_lengths, piece_shifts, own, received)

    distances, blocks, (new_first, new_second) = gather_tokens(ordered, (new_first, new_second))

    query_cols = HQ // lax.axis_size("tensor") * HS
    key_cols = block_cols - query_cols
    group_cols = P_LOW * GROUP_ROWS
    new_master, query, key = pl.pallas_call(
        functools.partial(product_kernel, distances),
        grid=(GROUPS,),
        out_shape=[
            state,
            jax.ShapeDtypeStruct((tokens_dev, query_cols), jnp.bfloat16),
            jax.ShapeDtypeStruct((tokens_dev, key_cols), jnp.bfloat16),
        ],
        in_specs=[SMEM] * 3
        + [pl.BlockSpec(memory_space=pl.ANY)]
        + [pl.BlockSpec((block.shape[0], group_cols), lambda g: (0, g)) for block in blocks],
        out_specs=[
            pl.BlockSpec((GROUP_ROWS, block_cols), lambda g: (g, 0)),
            pl.BlockSpec((tokens_dev, query_cols), lambda g: (0, 0)),
            pl.BlockSpec((tokens_dev, key_cols), lambda g: (0, 0)),
        ],
        scratch_shapes=[
            pltpu.VMEM((2 * NY, NX, NC, SLOTS, HS), jnp.bfloat16),
            pltpu.VMEM((N_DP, GROUP, HS), jnp.float32),
            pltpu.VMEM((N_Z * group_cols, block_cols), jnp.bfloat16),
            pltpu.VMEM((tokens_dev, block_cols), jnp.float32),
            pltpu.SMEM((N_DP,), jnp.int32),
            pltpu.SMEM((SLOTS // 16 + 8,), jnp.int32),
            pltpu.SemaphoreType.DMA((GROUPS, 2 * NX * NC)),
        ],
        compiler_params=pltpu.CompilerParams(vmem_limit_bytes=VMEM_LIMIT),
        cost_estimate=pl.CostEstimate(
            flops=2 * tokens_dev * width * N_Z * block_cols,
            bytes_accessed=2 * width * N_Z * (tokens_dev + block_cols),
            transcendentals=0,
        ),
        name="product",
    )(piece_lengths, piece_shifts, own, gathered, *blocks)
    return (new_master, new_first, new_second, query, key)


def solution(mesh):
    blocked = P("dp", "tensor")
    return jax.shard_map(
        per_device,
        mesh=mesh,
        in_specs=(blocked,) * 4 + (P(), P()),
        out_specs=(blocked,) * 5,
        check_vma=False,
    )
```

```python
import functools

import jax
import jax.numpy as jnp
from jax import lax
from jax.experimental import pallas as pl
from jax.experimental.pallas import tpu as pltpu
from jax.sharding import PartitionSpec as P

HQ = 48
HS = 128
NX = 4
NC = 2
HEADS = 7
ROWS = 96
SLOTS = ROWS * HEADS
HALF = SLOTS // 2
BUCKET = 16
N_DP = 64
NY = N_DP // (NX * NC)
GROUP_ROWS = 32
GROUP = GROUP_ROWS * HEADS
GROUPS = SLOTS // GROUP
CHUNK = 32
N_Z = 8
P_LOW = N_DP // N_Z
VMEM_LIMIT = 56 * 1024 * 1024


def dp_index(y, x, c):
    return (y * NX + x) * NC + c


X_GROUPS = [[dp_index(y, x, c) for x in range(NX)] for y in range(NY) for c in range(NC)]
Y_GROUPS = [[dp_index(y, x, c) for y in range(NY) for c in range(NC)] for x in range(NX)]


def pack_kernel(lengths, shifts, own, first, second, out, first_rows, second_rows):
    for rows, state in ((first_rows, first), (second_rows, second)):
        for head in range(HEADS):
            rows[pl.ds(head, ROWS, stride=HEADS), :] = state[:, head * HS : (head + 1) * HS]
        rows[SLOTS : SLOTS + BUCKET, :] = jnp.zeros((BUCKET, HS), jnp.float32)
    me = own[0]

    def piece(j, start):
        target = (me + shifts[j]) & (N_DP - 1)
        out[target, :, 0:HS] = first_rows[pl.ds(start, BUCKET), :].astype(jnp.bfloat16)
        out[target, :, HS : 2 * HS] = second_rows[pl.ds(start, BUCKET), :].astype(jnp.bfloat16)
        return start + lengths[j]

    lax.fori_loop(0, N_DP, piece, jnp.int32(0))


def unpack_kernel(lengths, shifts, own, received, first, second, first_rows, second_rows):
    me = own[0]

    def piece(j, start):
        source = (me - shifts[j]) & (N_DP - 1)
        first_rows[pl.ds(start, BUCKET), :] = received[source, :, 0:HS].astype(jnp.float32)
        second_rows[pl.ds(start, BUCKET), :] = received[source, :, HS : 2 * HS].astype(jnp.float32)
        return start + lengths[j]

    lax.fori_loop(0, N_DP, piece, jnp.int32(0))
    for rows, state in ((first_rows, first), (second_rows, second)):
        for head in range(HEADS):
            state[:, head * HS : (head + 1) * HS] = rows[pl.ds(head, ROWS, stride=HEADS), :]


def product_kernel(places, lengths, shifts, own, gathered, *refs):
    tokens, (master, query, key), (held, rows, weights, total, starts, firsts, sems) = refs[:-10], refs[-10:-7], refs[-7:]
    group = pl.program_id(0)
    me, my_z = own[0], own[1]
    blocks = held.reshape(2 * N_DP, SLOTS, HS)

    def copies(g):
        slots = pl.ds(pl.multiple_of(g * GROUP, GROUP), GROUP)
        return [
            pltpu.make_async_copy(
                gathered.at[:, c, x, slots, :],
                held.at[pl.ds(again * NY, NY), x, c, slots, :],
                sems.at[g, (again * NX + x) * NC + c],
            )
            for again in range(2)
            for x in range(NX)
            for c in range(NC)
        ]

    @pl.when(group == 0)
    def _():
        for g in range(GROUPS):
            for copy in copies(g):
                copy.start()

        def piece(j, start):
            starts[j] = start
            firsts[(start + 15) >> 4] = j
            return start + lengths[j]

        lax.fori_loop(0, N_DP, piece, jnp.int32(0))

    for copy in copies(group):
        copy.wait()

    sublane = lax.broadcasted_iota(jnp.int32, (16, HS), 0).astype(jnp.int16)

    def tile(t, carry):
        whole = group * (GROUP // 16) + t
        offset = pl.multiple_of(whole * 16, 16)
        begin, end = firsts[whole], firsts[whole + 1]

        def chunk(part, carry):
            def load(j):
                base = N_DP - shifts[j] + part * CHUNK
                return [blocks[base + i, pl.ds(offset, 16), :] for i in range(CHUNK)]

            def later(j, kept):
                take = sublane >= (starts[j] - offset).astype(jnp.int16)
                return [jnp.where(take, new, old) for new, old in zip(load(j), kept)]

            kept = lax.fori_loop(begin + 1, end + 1, later, load(begin))
            for i in range(CHUNK):
                rows[part * CHUNK + i, pl.ds(pl.multiple_of(t * 16, 16), 16), :] = kept[i].astype(jnp.float32)
            return carry

        return lax.fori_loop(0, N_DP // CHUNK, chunk, carry)

    lax.fori_loop(0, GROUP // 16, tile, jnp.int32(0))

    def spread(low, carry):
        for i, distance in enumerate(places):
            p = ((my_z + distance) & (N_Z - 1)) * P_LOW + low
            at = pl.ds(pl.multiple_of((i * P_LOW + low) * GROUP_ROWS, GROUP_ROWS), GROUP_ROWS)
            for head in range(HEADS):
                weights[at, head * HS : (head + 1) * HS] = rows[p, pl.ds(head, GROUP_ROWS, stride=HEADS), :].astype(
                    jnp.bfloat16
                )
        return carry

    lax.fori_loop(0, P_LOW, spread, jnp.int32(0))
    for head in range(HEADS):
        master[:, head * HS : (head + 1) * HS] = rows[me, pl.ds(head, GROUP_ROWS, stride=HEADS), :]

    last = jnp.concatenate([tokens[-2][...], tokens[-1][...]], axis=0)
    columns = jnp.concatenate([block[...] for block in tokens[:-2]] + [last], axis=1)
    part = jnp.dot(columns, weights[...], preferred_element_type=jnp.float32)

    @pl.when(group == 0)
    def _():
        total[...] = part

    @pl.when(group > 0)
    def _():
        total[...] += part

    @pl.when(group == pl.num_programs(0) - 1)
    def _():
        query[...] = total[:, : query.shape[1]].astype(query.dtype)
        key[...] = total[:, query.shape[1] :].astype(key.dtype)


SMEM = pl.BlockSpec(memory_space=pltpu.SMEM)
VMEM = pl.BlockSpec(memory_space=pltpu.VMEM)


def gather_tokens(tokens):
    up = [(z, (z + 1) % N_Z) for z in range(N_Z)]
    down = [(z, (z - 1) % N_Z) for z in range(N_Z)]
    half = tokens.shape[0] // 2
    from_below, from_above = tokens, tokens
    distances, arrays = [0], [tokens]
    for distance in range(1, N_Z // 2):
        from_below = lax.ppermute(from_below, "tensor", up)
        from_above = lax.ppermute(from_above, "tensor", down)
        distances += [-distance, distance]
        arrays += [from_below, from_above]
    distances.append(N_Z // 2)
    arrays.append(lax.ppermute(from_below[:half], "tensor", up))
    arrays.append(lax.ppermute(from_above[half:], "tensor", down))
    return tuple(distances), arrays


def per_device(tokens, old_master, old_first, old_second, piece_lengths, piece_shifts):
    own = jnp.stack([lax.axis_index("dp"), lax.axis_index("tensor")]).astype(jnp.int32)
    depth_dev, block_cols = old_master.shape
    state = jax.ShapeDtypeStruct((depth_dev, block_cols), jnp.float32)
    slots = pltpu.VMEM((SLOTS + BUCKET, HS), jnp.float32)

    column = old_master.astype(jnp.bfloat16).reshape(SLOTS, HS)
    row = lax.all_gather(column, "dp", axis_index_groups=X_GROUPS, axis=0, tiled=True)
    gathered = lax.all_gather(row, "dp", axis_index_groups=Y_GROUPS, axis=0, tiled=True)
    gathered = gathered.reshape(NY, NC, NX, SLOTS, HS)

    tokens_dev, width = tokens.shape
    old = jnp.arange(width, dtype=jnp.int32)
    low, depth = old // depth_dev, old % depth_dev
    new = (depth // GROUP_ROWS * P_LOW + low) * GROUP_ROWS + depth % GROUP_ROWS
    order = (new[:, None] == old[None, :]).astype(jnp.bfloat16)
    ordered = jnp.dot(tokens, order, preferred_element_type=jnp.float32).astype(jnp.bfloat16)
    packed = pl.pallas_call(
        pack_kernel,
        out_shape=jax.ShapeDtypeStruct((N_DP, BUCKET, 2 * HS), jnp.bfloat16),
        in_specs=[SMEM] * 3 + [VMEM] * 2,
        out_specs=VMEM,
        scratch_shapes=[slots, slots],
        name="pack",
    )(piece_lengths, piece_shifts, own, old_first, old_second)
    distances, blocks = gather_tokens(ordered)
    packed, blocks = lax.optimization_barrier((packed, blocks))
    received = lax.all_to_all(packed, "dp", split_axis=0, concat_axis=0, tiled=True)

    query_cols = HQ // lax.axis_size("tensor") * HS
    key_cols = block_cols - query_cols
    group_cols = P_LOW * GROUP_ROWS
    new_master, query, key = pl.pallas_call(
        functools.partial(product_kernel, distances),
        grid=(GROUPS,),
        out_shape=[
            state,
            jax.ShapeDtypeStruct((tokens_dev, query_cols), jnp.bfloat16),
            jax.ShapeDtypeStruct((tokens_dev, key_cols), jnp.bfloat16),
        ],
        in_specs=[SMEM] * 3
        + [pl.BlockSpec(memory_space=pl.ANY)]
        + [pl.BlockSpec((block.shape[0], group_cols), lambda g: (0, g)) for block in blocks],
        out_specs=[
            pl.BlockSpec((GROUP_ROWS, block_cols), lambda g: (g, 0)),
            pl.BlockSpec((tokens_dev, query_cols), lambda g: (0, 0)),
            pl.BlockSpec((tokens_dev, key_cols), lambda g: (0, 0)),
        ],
        scratch_shapes=[
            pltpu.VMEM((2 * NY, NX, NC, SLOTS, HS), jnp.bfloat16),
            pltpu.VMEM((N_DP, GROUP, HS), jnp.float32),
            pltpu.VMEM((N_Z * group_cols, block_cols), jnp.bfloat16),
            pltpu.VMEM((tokens_dev, block_cols), jnp.float32),
            pltpu.SMEM((N_DP,), jnp.int32),
            pltpu.SMEM((SLOTS // 16 + 8,), jnp.int32),
            pltpu.SemaphoreType.DMA((GROUPS, 2 * NX * NC)),
        ],
        compiler_params=pltpu.CompilerParams(vmem_limit_bytes=VMEM_LIMIT),
        cost_estimate=pl.CostEstimate(
            flops=2 * tokens_dev * width * N_Z * block_cols,
            bytes_accessed=2 * width * N_Z * (tokens_dev + block_cols),
            transcendentals=0,
        ),
        name="product",
    )(piece_lengths, piece_shifts, own, gathered, *blocks)
    received, key = lax.optimization_barrier((received, key))
    new_first, new_second = pl.pallas_call(
        unpack_kernel,
        out_shape=[state, state],
        in_specs=[SMEM] * 3 + [VMEM],
        out_specs=[VMEM] * 2,
        scratch_shapes=[slots, slots],
        name="unpack",
    )(piece_lengths, piece_shifts, own, received)
    return (new_master, new_first, new_second, query, key)


def solution(mesh):
    blocked = P("dp", "tensor")
    return jax.shard_map(
        per_device,
        mesh=mesh,
        in_specs=(blocked,) * 4 + (P(), P()),
        out_specs=(blocked,) * 5,
        check_vma=False,
    )
```

```python
import functools

import jax
import jax.numpy as jnp
from jax import lax
from jax.experimental import pallas as pl
from jax.experimental.pallas import tpu as pltpu
from jax.sharding import PartitionSpec as P

HQ = 48
HS = 128
NX = 4
NC = 2
HEADS = 7
ROWS = 96
SLOTS = ROWS * HEADS
HALF = SLOTS // 2
BUCKET = 16
N_DP = 64
NY = N_DP // (NX * NC)
GROUP_ROWS = 32
GROUP = GROUP_ROWS * HEADS
GROUPS = SLOTS // GROUP
CHUNK = 32
N_Z = 8
P_LOW = N_DP // N_Z
VMEM_LIMIT = 56 * 1024 * 1024


def dp_moves(dy, dx, dc):
    moves = []
    for y in range(NY):
        for x in range(NX):
            for c in range(NC):
                source = (y * NX + x) * NC + c
                target = ((y + dy) % NY * NX + (x + dx) % NX) * NC + (c + dc) % NC
                moves.append((source, target))
    return moves


X_UP, X_DOWN = dp_moves(0, 1, 0), dp_moves(0, -1, 0)
Y_UP, Y_DOWN = dp_moves(1, 0, 0), dp_moves(-1, 0, 0)
SIBLING = dp_moves(0, 0, 1)


def move(array, moves):
    return lax.ppermute(array, "dp", moves)


def pack_kernel(lengths, shifts, own, first, second, out, first_rows, second_rows):
    for rows, state in ((first_rows, first), (second_rows, second)):
        for head in range(HEADS):
            rows[pl.ds(head, ROWS, stride=HEADS), :] = state[:, head * HS : (head + 1) * HS]
        rows[SLOTS : SLOTS + BUCKET, :] = jnp.zeros((BUCKET, HS), jnp.float32)
    me = own[0]

    def piece(j, start):
        target = (me + shifts[j]) & (N_DP - 1)
        out[target, :, 0:HS] = first_rows[pl.ds(start, BUCKET), :].astype(jnp.bfloat16)
        out[target, :, HS : 2 * HS] = second_rows[pl.ds(start, BUCKET), :].astype(jnp.bfloat16)
        return start + lengths[j]

    lax.fori_loop(0, N_DP, piece, jnp.int32(0))


def unpack_kernel(lengths, shifts, own, received, first, second, first_rows, second_rows):
    me = own[0]

    def piece(j, start):
        source = (me - shifts[j]) & (N_DP - 1)
        first_rows[pl.ds(start, BUCKET), :] = received[source, :, 0:HS].astype(jnp.float32)
        second_rows[pl.ds(start, BUCKET), :] = received[source, :, HS : 2 * HS].astype(jnp.float32)
        return start + lengths[j]

    lax.fori_loop(0, N_DP, piece, jnp.int32(0))
    for rows, state in ((first_rows, first), (second_rows, second)):
        for head in range(HEADS):
            state[:, head * HS : (head + 1) * HS] = rows[pl.ds(head, ROWS, stride=HEADS), :]


def product_kernel(places, spans, lengths, shifts, own, *refs):
    n = len(spans)
    gathered, tokens, (master, query, key) = refs[:n], refs[n:-10], refs[-10:-7]
    blocks, rows, weights, total, starts, firsts, sems = refs[-7:]
    group = pl.program_id(0)
    me, my_z = own[0], own[1]
    my_y, my_x, my_c = me // (NX * NC), (me // NC) % NX, me % NC

    def copies(g):
        slots = pl.ds(pl.multiple_of(g * GROUP, GROUP), GROUP)
        return [
            pltpu.make_async_copy(
                gathered[i].at[:, slots, :],
                blocks.at[low, pl.ds(again * NY + at, count), slots, :],
                sems.at[g, again * n + i],
            )
            for again in range(2)
            for i, (low, at, count) in enumerate(spans)
        ]

    @pl.when(group == 0)
    def _():
        for g in range(GROUPS):
            for copy in copies(g):
                copy.start()

        def piece(j, start):
            starts[j] = start
            firsts[(start + 15) >> 4] = j
            return start + lengths[j]

        lax.fori_loop(0, N_DP, piece, jnp.int32(0))

    for copy in copies(group):
        copy.wait()

    sublane = lax.broadcasted_iota(jnp.int32, (16, HS), 0).astype(jnp.int16)

    def tile(t, carry):
        whole = group * (GROUP // 16) + t
        offset = pl.multiple_of(whole * 16, 16)
        begin, end = firsts[whole], firsts[whole + 1]

        def chunk(part, carry):
            def load(j):
                found = []
                for u in range(CHUNK // NY):
                    low = part * (CHUNK // NY) + u
                    low_from = (low - shifts[j]) & (NX * NC - 1)
                    borrow = jnp.where(low < (shifts[j] & (NX * NC - 1)), 1, 0)
                    y_from = (0 - (shifts[j] >> 3) - borrow - my_y) & (NY - 1)
                    place = (((low_from >> 1) - my_x) & (NX - 1)) * NC + ((low_from - my_c) & (NC - 1))
                    found += [blocks[place, y_from + i, pl.ds(offset, 16), :] for i in range(NY)]
                return found

            def later(j, kept):
                take = sublane >= (starts[j] - offset).astype(jnp.int16)
                return [jnp.where(take, new, old) for new, old in zip(load(j), kept)]

            kept = lax.fori_loop(begin + 1, end + 1, later, load(begin))
            for i in range(CHUNK):
                p = i % NY * (NX * NC) + part * (CHUNK // NY) + i // NY
                rows[p, pl.ds(pl.multiple_of(t * 16, 16), 16), :] = kept[i].astype(jnp.float32)
            return carry

        return lax.fori_loop(0, N_DP // CHUNK, chunk, carry)

    lax.fori_loop(0, GROUP // 16, tile, jnp.int32(0))

    def spread(low, carry):
        for i, distance in enumerate(places):
            p = ((my_z + distance) & (N_Z - 1)) * P_LOW + low
            at = pl.ds(pl.multiple_of((i * P_LOW + low) * GROUP_ROWS, GROUP_ROWS), GROUP_ROWS)
            for head in range(HEADS):
                weights[at, head * HS : (head + 1) * HS] = rows[p, pl.ds(head, GROUP_ROWS, stride=HEADS), :].astype(
                    jnp.bfloat16
                )
        return carry

    lax.fori_loop(0, P_LOW, spread, jnp.int32(0))
    for head in range(HEADS):
        master[:, head * HS : (head + 1) * HS] = rows[me, pl.ds(head, GROUP_ROWS, stride=HEADS), :]

    last = jnp.concatenate([tokens[-2][...], tokens[-1][...]], axis=0)
    columns = jnp.concatenate([block[...] for block in tokens[:-2]] + [last], axis=1)
    part = jnp.dot(columns, weights[...], preferred_element_type=jnp.float32)

    @pl.when(group == 0)
    def _():
        total[...] = part

    @pl.when(group > 0)
    def _():
        total[...] += part

    @pl.when(group == pl.num_programs(0) - 1)
    def _():
        query[...] = total[:, : query.shape[1]].astype(query.dtype)
        key[...] = total[:, query.shape[1] :].astype(key.dtype)


SMEM = pl.BlockSpec(memory_space=pltpu.SMEM)
VMEM = pl.BlockSpec(memory_space=pltpu.VMEM)


def gather_master(block):
    ups, downs = [block], [block]
    for _ in range(NY // 2 - 1):
        ups.append(move(ups[-1], Y_UP))
        downs.append(move(downs[-1], Y_DOWN))
    column = jnp.concatenate(downs + [move(ups[-1], Y_UP)] + ups[:0:-1], axis=0)
    from_below, from_above = move(column, X_UP), move(column, X_DOWN)
    half = NY // 2
    parts = [
        (0, 0, column),
        (3, 0, from_below),
        (1, 0, from_above),
        (2, 0, move(from_below[:half], X_UP)),
        (2, half, move(from_above[half:], X_DOWN)),
    ]
    parts = [(dx * NC, at, part) for dx, at, part in parts] + [
        (dx * NC + 1, at, move(part, SIBLING)) for dx, at, part in parts
    ]
    return tuple((low, at, part.shape[0]) for low, at, part in parts), [part for _, _, part in parts]


def gather_tokens(tokens, packed, exchange):
    up = [(z, (z + 1) % N_Z) for z in range(N_Z)]
    down = [(z, (z - 1) % N_Z) for z in range(N_Z)]
    half = tokens.shape[0] // 2
    from_below, from_above = tokens, tokens
    distances, arrays = [0], [tokens]
    for distance in range(1, N_Z // 2):
        from_below = lax.ppermute(from_below, "tensor", up)
        from_above = lax.ppermute(from_above, "tensor", down)
        distances += [-distance, distance]
        if distance == 2:
            from_below, from_above, packed = lax.optimization_barrier((from_below, from_above, packed))
            moments = exchange(packed)
        if distance == 3:
            from_below, from_above, moments = lax.optimization_barrier((from_below, from_above, moments))
        arrays += [from_below, from_above]
    distances.append(N_Z // 2)
    arrays.append(lax.ppermute(from_below[:half], "tensor", up))
    arrays.append(lax.ppermute(from_above[half:], "tensor", down))
    return tuple(distances), arrays, moments


def per_device(tokens, old_master, old_first, old_second, piece_lengths, piece_shifts):
    own = jnp.stack([lax.axis_index("dp"), lax.axis_index("tensor")]).astype(jnp.int32)
    depth_dev, block_cols = old_master.shape
    state = jax.ShapeDtypeStruct((depth_dev, block_cols), jnp.float32)
    slots = pltpu.VMEM((SLOTS + BUCKET, HS), jnp.float32)

    column = old_master.astype(jnp.bfloat16).reshape(SLOTS, HS)
    spans, gathered = gather_master(column[None])

    tokens_dev, width = tokens.shape
    old = jnp.arange(width, dtype=jnp.int32)
    low, depth = old // depth_dev, old % depth_dev
    new = (depth // GROUP_ROWS * P_LOW + low) * GROUP_ROWS + depth % GROUP_ROWS
    order = (new[:, None] == old[None, :]).astype(jnp.bfloat16)
    ordered = jnp.dot(tokens, order, preferred_element_type=jnp.float32).astype(jnp.bfloat16)
    packed = pl.pallas_call(
        pack_kernel,
        out_shape=jax.ShapeDtypeStruct((N_DP, BUCKET, 2 * HS), jnp.bfloat16),
        in_specs=[SMEM] * 3 + [VMEM] * 2,
        out_specs=VMEM,
        scratch_shapes=[slots, slots],
        name="pack",
    )(piece_lengths, piece_shifts, own, old_first, old_second)
    def exchange(packed):
        received = lax.all_to_all(packed, "dp", split_axis=0, concat_axis=0, tiled=True)
        return pl.pallas_call(
            unpack_kernel,
            out_shape=[state, state],
            in_specs=[SMEM] * 3 + [VMEM],
            out_specs=[VMEM] * 2,
            scratch_shapes=[slots, slots],
            name="unpack",
        )(piece_lengths, piece_shifts, own, received)

    distances, blocks, (new_first, new_second) = gather_tokens(ordered, packed, exchange)

    query_cols = HQ // lax.axis_size("tensor") * HS
    key_cols = block_cols - query_cols
    group_cols = P_LOW * GROUP_ROWS
    new_master, query, key = pl.pallas_call(
        functools.partial(product_kernel, distances, spans),
        grid=(GROUPS,),
        out_shape=[
            state,
            jax.ShapeDtypeStruct((tokens_dev, query_cols), jnp.bfloat16),
            jax.ShapeDtypeStruct((tokens_dev, key_cols), jnp.bfloat16),
        ],
        in_specs=[SMEM] * 3
        + [pl.BlockSpec(memory_space=pl.ANY)] * len(gathered)
        + [pl.BlockSpec((block.shape[0], group_cols), lambda g: (0, g)) for block in blocks],
        out_specs=[
            pl.BlockSpec((GROUP_ROWS, block_cols), lambda g: (g, 0)),
            pl.BlockSpec((tokens_dev, query_cols), lambda g: (0, 0)),
            pl.BlockSpec((tokens_dev, key_cols), lambda g: (0, 0)),
        ],
        scratch_shapes=[
            pltpu.VMEM((NX * NC, 2 * NY, SLOTS, HS), jnp.bfloat16),
            pltpu.VMEM((N_DP, GROUP, HS), jnp.float32),
            pltpu.VMEM((N_Z * group_cols, block_cols), jnp.bfloat16),
            pltpu.VMEM((tokens_dev, block_cols), jnp.float32),
            pltpu.SMEM((N_DP,), jnp.int32),
            pltpu.SMEM((SLOTS // 16 + 8,), jnp.int32),
            pltpu.SemaphoreType.DMA((GROUPS, 2 * len(gathered))),
        ],
        compiler_params=pltpu.CompilerParams(vmem_limit_bytes=VMEM_LIMIT),
        cost_estimate=pl.CostEstimate(
            flops=2 * tokens_dev * width * N_Z * block_cols,
            bytes_accessed=2 * width * N_Z * (tokens_dev + block_cols),
            transcendentals=0,
        ),
        name="product",
    )(piece_lengths, piece_shifts, own, *gathered, *blocks)
    return (new_master, new_first, new_second, query, key)


def solution(mesh):
    blocked = P("dp", "tensor")
    return jax.shard_map(
        per_device,
        mesh=mesh,
        in_specs=(blocked,) * 4 + (P(), P()),
        out_specs=(blocked,) * 5,
        check_vma=False,
    )
```

```python
import functools

import jax
import jax.numpy as jnp
from jax import lax
from jax.experimental import pallas as pl
from jax.experimental.pallas import tpu as pltpu
from jax.sharding import PartitionSpec as P

HQ = 48
HS = 128
NX = 4
NC = 2
HEADS = 7
ROWS = 96
SLOTS = ROWS * HEADS
HALF = SLOTS // 2
BUCKET = 16
N_DP = 64
NY = N_DP // (NX * NC)
GROUP_ROWS = 32
GROUP = GROUP_ROWS * HEADS
GROUPS = SLOTS // GROUP
STEP = 112
CHUNK = 32
N_Z = 8
P_LOW = N_DP // N_Z
VMEM_LIMIT = 56 * 1024 * 1024


def dp_index(y, x, c):
    return (y * NX + x) * NC + c


X_GROUPS = [[dp_index(y, x, c) for x in range(NX)] for y in range(NY) for c in range(NC)]
Y_GROUPS = [[dp_index(y, x, c) for y in range(NY) for c in range(NC)] for x in range(NX)]


def pack_kernel(lengths, shifts, own, first, second, out, first_rows, second_rows):
    for rows, state in ((first_rows, first), (second_rows, second)):
        for head in range(HEADS):
            rows[pl.ds(head, ROWS, stride=HEADS), :] = state[:, head * HS : (head + 1) * HS]
        rows[SLOTS : SLOTS + BUCKET, :] = jnp.zeros((BUCKET, HS), jnp.float32)
    me = own[0]

    def piece(j, start):
        target = (me + shifts[j]) & (N_DP - 1)
        out[target, :, 0:HS] = first_rows[pl.ds(start, BUCKET), :].astype(jnp.bfloat16)
        out[target, :, HS : 2 * HS] = second_rows[pl.ds(start, BUCKET), :].astype(jnp.bfloat16)
        return start + lengths[j]

    lax.fori_loop(0, N_DP, piece, jnp.int32(0))


def unpack_kernel(lengths, shifts, own, received, first, second, first_rows, second_rows):
    me = own[0]

    def piece(j, start):
        source = (me - shifts[j]) & (N_DP - 1)
        first_rows[pl.ds(start, BUCKET), :] = received[source, :, 0:HS].astype(jnp.float32)
        second_rows[pl.ds(start, BUCKET), :] = received[source, :, HS : 2 * HS].astype(jnp.float32)
        return start + lengths[j]

    lax.fori_loop(0, N_DP, piece, jnp.int32(0))
    for rows, state in ((first_rows, first), (second_rows, second)):
        for head in range(HEADS):
            state[:, head * HS : (head + 1) * HS] = rows[pl.ds(head, ROWS, stride=HEADS), :]


def product_kernel(places, lengths, shifts, own, gathered, *refs):
    tokens, (master, query, key), (held, columns, rows, weights, total, starts, firsts, sems, token_sems) = (
        refs[:-12],
        refs[-12:-9],
        refs[-9:],
    )
    me, my_z = own[0], own[1]
    blocks = held.reshape(N_DP + CHUNK, SLOTS, HS)
    half = tokens[-1].shape[0]

    def copies(step):
        slots = pl.ds(step * STEP, STEP)
        return [
            pltpu.make_async_copy(
                gathered.at[pl.ds(0, count), c, :, slots, :],
                held.at[pl.ds(at, count), :, c, slots, :],
                sems.at[step, again * NC + c],
            )
            for again, (at, count) in enumerate(((0, NY), (NY, CHUNK // (NX * NC))))
            for c in range(NC)
        ]

    def token_copies(group):
        wide = P_LOW * GROUP_ROWS
        found = []
        for i, block in enumerate(tokens):
            last = i == len(tokens) - 1
            found.append(
                pltpu.make_async_copy(
                    block.at[:, pl.ds(group * wide, wide)],
                    columns.at[
                        group, pl.ds(half if last else 0, block.shape[0]), pl.ds((i - 1 if last else i) * wide, wide)
                    ],
                    token_sems.at[group, i],
                )
            )
        return found

    per_group = GROUP // STEP
    for group in range(GROUPS):
        for step in range(group * per_group, (group + 1) * per_group):
            for copy in copies(step):
                copy.start()
        for copy in token_copies(group):
            copy.start()

    def piece(j, start):
        starts[j] = start
        firsts[(start + 15) >> 4] = j
        return start + lengths[j]

    lax.fori_loop(0, N_DP, piece, jnp.int32(0))
    sublane = lax.broadcasted_iota(jnp.int32, (16, HS), 0).astype(jnp.int16)

    def select(group, step):
        def tile(t, carry):
            whole = step * (STEP // 16) + t
            offset = pl.multiple_of(whole * 16, 16)
            at = pl.ds(pl.multiple_of(offset - group * GROUP, 16), 16)
            begin, end = firsts[whole], firsts[whole + 1]

            def chunk(part, carry):
                def load(j):
                    base = (part * CHUNK - shifts[j]) & (N_DP - 1)
                    return [blocks[base + i, pl.ds(offset, 16), :] for i in range(CHUNK)]

                def later(j, kept):
                    take = sublane >= (starts[j] - offset).astype(jnp.int16)
                    return [jnp.where(take, new, old) for new, old in zip(load(j), kept)]

                kept = lax.fori_loop(begin + 1, end + 1, later, load(begin))
                for i in range(CHUNK):
                    rows[part * CHUNK + i, at, :] = kept[i].astype(jnp.float32)
                return carry

            return lax.fori_loop(0, N_DP // CHUNK, chunk, carry)

        lax.fori_loop(0, STEP // 16, tile, jnp.int32(0))

    def spread(low, carry):
        for i, distance in enumerate(places):
            p = ((my_z + distance) & (N_Z - 1)) * P_LOW + low
            at = pl.ds(pl.multiple_of((i * P_LOW + low) * GROUP_ROWS, GROUP_ROWS), GROUP_ROWS)
            for head in range(HEADS):
                weights[at, head * HS : (head + 1) * HS] = rows[
                    p, pl.ds(head, GROUP_ROWS, stride=HEADS), :
                ].astype(jnp.bfloat16)
        return carry

    def one_group(group, carry):
        def one_step(step, carry):
            for copy in copies(group * per_group + step):
                copy.wait()
            select(group, group * per_group + step)
            return carry

        lax.fori_loop(0, per_group, one_step, jnp.int32(0))
        lax.fori_loop(0, P_LOW, spread, jnp.int32(0))
        for head in range(HEADS):
            master[pl.ds(pl.multiple_of(group * GROUP_ROWS, GROUP_ROWS), GROUP_ROWS), head * HS : (head + 1) * HS] = rows[
                me, pl.ds(head, GROUP_ROWS, stride=HEADS), :
            ]
        for copy in token_copies(group):
            copy.wait()
        part = jnp.dot(columns[group], weights[...], preferred_element_type=jnp.float32)

        @pl.when(group == 0)
        def _():
            total[...] = part

        @pl.when(group > 0)
        def _():
            total[...] += part

        return carry

    lax.fori_loop(0, GROUPS, one_group, jnp.int32(0))
    cols = query.shape[1]
    query[...] = total[:, :cols].astype(query.dtype)
    key[...] = total[:, cols:].astype(key.dtype)


SMEM = pl.BlockSpec(memory_space=pltpu.SMEM)
VMEM = pl.BlockSpec(memory_space=pltpu.VMEM)


def gather_tokens(tokens, moments):
    up = [(z, (z + 1) % N_Z) for z in range(N_Z)]
    down = [(z, (z - 1) % N_Z) for z in range(N_Z)]
    half = tokens.shape[0] // 2
    from_below, from_above = tokens, tokens
    distances, arrays = [0], [tokens]
    for distance in range(1, N_Z // 2):
        from_below = lax.ppermute(from_below, "tensor", up)
        from_above = lax.ppermute(from_above, "tensor", down)
        distances += [-distance, distance]
        if distance == 2:
            from_below, from_above, moments = lax.optimization_barrier((from_below, from_above, moments))
        arrays += [from_below, from_above]
    distances.append(N_Z // 2)
    arrays.append(lax.ppermute(from_below[:half], "tensor", up))
    arrays.append(lax.ppermute(from_above[half:], "tensor", down))
    return tuple(distances), arrays, moments


def per_device(tokens, old_master, old_first, old_second, piece_lengths, piece_shifts):
    own = jnp.stack([lax.axis_index("dp"), lax.axis_index("tensor")]).astype(jnp.int32)
    depth_dev, block_cols = old_master.shape
    state = jax.ShapeDtypeStruct((depth_dev, block_cols), jnp.float32)
    slots = pltpu.VMEM((SLOTS + BUCKET, HS), jnp.float32)

    column = old_master.astype(jnp.bfloat16).reshape(SLOTS, HS)
    row = lax.all_gather(column, "dp", axis_index_groups=X_GROUPS, axis=0, tiled=True)
    gathered = lax.all_gather(row, "dp", axis_index_groups=Y_GROUPS, axis=0, tiled=True)
    gathered = gathered.reshape(NY, NC, NX, SLOTS, HS)

    tokens_dev, width = tokens.shape
    old = jnp.arange(width, dtype=jnp.int32)
    low, depth = old // depth_dev, old % depth_dev
    new = (depth // GROUP_ROWS * P_LOW + low) * GROUP_ROWS + depth % GROUP_ROWS
    order = (new[:, None] == old[None, :]).astype(jnp.bfloat16)
    ordered = jnp.dot(tokens, order, preferred_element_type=jnp.float32).astype(jnp.bfloat16)
    packed = pl.pallas_call(
        pack_kernel,
        out_shape=jax.ShapeDtypeStruct((N_DP, BUCKET, 2 * HS), jnp.bfloat16),
        in_specs=[SMEM] * 3 + [VMEM] * 2,
        out_specs=VMEM,
        scratch_shapes=[slots, slots],
        name="pack",
    )(piece_lengths, piece_shifts, own, old_first, old_second)
    received = lax.all_to_all(packed, "dp", split_axis=0, concat_axis=0, tiled=True)
    new_first, new_second = pl.pallas_call(
        unpack_kernel,
        out_shape=[state, state],
        in_specs=[SMEM] * 3 + [VMEM],
        out_specs=[VMEM] * 2,
        scratch_shapes=[slots, slots],
        name="unpack",
    )(piece_lengths, piece_shifts, own, received)

    distances, blocks, (new_first, new_second) = gather_tokens(ordered, (new_first, new_second))

    query_cols = HQ // lax.axis_size("tensor") * HS
    key_cols = block_cols - query_cols
    group_cols = P_LOW * GROUP_ROWS
    new_master, query, key = pl.pallas_call(
        functools.partial(product_kernel, distances),
        out_shape=[
            state,
            jax.ShapeDtypeStruct((tokens_dev, query_cols), jnp.bfloat16),
            jax.ShapeDtypeStruct((tokens_dev, key_cols), jnp.bfloat16),
        ],
        in_specs=[SMEM] * 3 + [pl.BlockSpec(memory_space=pl.ANY)] * (1 + len(blocks)),
        out_specs=[VMEM] * 3,
        scratch_shapes=[
            pltpu.VMEM((NY + CHUNK // (NX * NC), NX, NC, SLOTS, HS), jnp.bfloat16),
            pltpu.VMEM((GROUPS, tokens_dev, N_Z * group_cols), jnp.bfloat16),
            pltpu.VMEM((N_DP, GROUP, HS), jnp.float32),
            pltpu.VMEM((N_Z * group_cols, block_cols), jnp.bfloat16),
            pltpu.VMEM((tokens_dev, block_cols), jnp.float32),
            pltpu.SMEM((N_DP,), jnp.int32),
            pltpu.SMEM((SLOTS // 16 + 8,), jnp.int32),
            pltpu.SemaphoreType.DMA((SLOTS // STEP, 2 * NC)),
            pltpu.SemaphoreType.DMA((GROUPS, len(blocks))),
        ],
        compiler_params=pltpu.CompilerParams(vmem_limit_bytes=VMEM_LIMIT),
        cost_estimate=pl.CostEstimate(
            flops=2 * tokens_dev * width * N_Z * block_cols,
            bytes_accessed=2 * width * N_Z * (tokens_dev + block_cols),
            transcendentals=0,
        ),
        name="product",
    )(piece_lengths, piece_shifts, own, gathered, *blocks)
    return (new_master, new_first, new_second, query, key)


def solution(mesh):
    blocked = P("dp", "tensor")
    return jax.shard_map(
        per_device,
        mesh=mesh,
        in_specs=(blocked,) * 4 + (P(), P()),
        out_specs=(blocked,) * 5,
        check_vma=False,
    )
```

```python
import functools

import jax
import jax.numpy as jnp
from jax import lax
from jax.experimental import pallas as pl
from jax.experimental.pallas import tpu as pltpu
from jax.sharding import PartitionSpec as P

HQ = 48
HS = 128
NX = 4
NC = 2
HEADS = 7
ROWS = 96
SLOTS = ROWS * HEADS
HALF = SLOTS // 2
BUCKET = 16
N_DP = 64
NY = N_DP // (NX * NC)
GROUP_ROWS = 32
GROUP = GROUP_ROWS * HEADS
GROUPS = SLOTS // GROUP
STEP = 112
CHUNK = 32
N_Z = 8
P_LOW = N_DP // N_Z
VMEM_LIMIT = 56 * 1024 * 1024


def dp_index(y, x, c):
    return (y * NX + x) * NC + c


X_GROUPS = [[dp_index(y, x, c) for x in range(NX)] for y in range(NY) for c in range(NC)]
Y_GROUPS = [[dp_index(y, x, c) for y in range(NY) for c in range(NC)] for x in range(NX)]


def pack_kernel(lengths, shifts, own, first, second, out, first_rows, second_rows):
    for rows, state in ((first_rows, first), (second_rows, second)):
        for head in range(HEADS):
            rows[pl.ds(head, ROWS, stride=HEADS), :] = state[:, head * HS : (head + 1) * HS]
        rows[SLOTS : SLOTS + BUCKET, :] = jnp.zeros((BUCKET, HS), jnp.float32)
    me = own[0]

    def piece(j, start):
        target = (me + shifts[j]) & (N_DP - 1)
        out[target, :, 0:HS] = first_rows[pl.ds(start, BUCKET), :].astype(jnp.bfloat16)
        out[target, :, HS : 2 * HS] = second_rows[pl.ds(start, BUCKET), :].astype(jnp.bfloat16)
        return start + lengths[j]

    lax.fori_loop(0, N_DP, piece, jnp.int32(0))


def unpack_kernel(lengths, shifts, own, received, first, second, first_rows, second_rows):
    me = own[0]

    def piece(j, start):
        source = (me - shifts[j]) & (N_DP - 1)
        first_rows[pl.ds(start, BUCKET), :] = received[source, :, 0:HS].astype(jnp.float32)
        second_rows[pl.ds(start, BUCKET), :] = received[source, :, HS : 2 * HS].astype(jnp.float32)
        return start + lengths[j]

    lax.fori_loop(0, N_DP, piece, jnp.int32(0))
    for rows, state in ((first_rows, first), (second_rows, second)):
        for head in range(HEADS):
            state[:, head * HS : (head + 1) * HS] = rows[pl.ds(head, ROWS, stride=HEADS), :]


def product_kernel(places, lengths, shifts, own, gathered, *refs):
    tokens, (master, query, key), (held, columns, rows, weights, total, starts, firsts, sems, token_sems) = (
        refs[:-12],
        refs[-12:-9],
        refs[-9:],
    )
    me, my_z = own[0], own[1]
    blocks = held.reshape(N_DP + CHUNK, SLOTS, HS)
    half = tokens[-1].shape[0]

    def copies(step):
        slots = pl.ds(step * STEP, STEP)
        return [
            pltpu.make_async_copy(
                gathered.at[pl.ds(0, count), c, :, slots, :],
                held.at[pl.ds(at, count), :, c, slots, :],
                sems.at[step, again * NC + c],
            )
            for again, (at, count) in enumerate(((0, NY), (NY, CHUNK // (NX * NC))))
            for c in range(NC)
        ]

    def token_copies(group):
        wide = P_LOW * GROUP_ROWS
        found = []
        for i, block in enumerate(tokens):
            last = i == len(tokens) - 1
            found.append(
                pltpu.make_async_copy(
                    block.at[:, pl.ds(group * wide, wide)],
                    columns.at[
                        group, pl.ds(half if last else 0, block.shape[0]), pl.ds((i - 1 if last else i) * wide, wide)
                    ],
                    token_sems.at[group, i],
                )
            )
        return found

    per_group = GROUP // STEP
    for group in range(GROUPS):
        for step in range(group * per_group, (group + 1) * per_group):
            for copy in copies(step):
                copy.start()
        for copy in token_copies(group):
            copy.start()

    def piece(j, start):
        starts[j] = start
        firsts[(start + 15) >> 4] = j
        return start + lengths[j]

    lax.fori_loop(0, N_DP, piece, jnp.int32(0))
    sublane = lax.broadcasted_iota(jnp.int32, (16, HS), 0).astype(jnp.int16)

    def select(group, step):
        def tile(t, carry):
            whole = step * (STEP // 16) + t
            offset = pl.multiple_of(whole * 16, 16)
            at = pl.ds(pl.multiple_of(offset - group * GROUP, 16), 16)
            begin, end = firsts[whole], firsts[whole + 1]

            def chunk(part, carry):
                def load(j):
                    base = (part * CHUNK - shifts[j]) & (N_DP - 1)
                    return [blocks[base + i, pl.ds(offset, 16), :] for i in range(CHUNK)]

                def later(j, kept):
                    take = sublane >= (starts[j] - offset).astype(jnp.int16)
                    return [jnp.where(take, new, old) for new, old in zip(load(j), kept)]

                kept = lax.fori_loop(begin + 1, end + 1, later, load(begin))
                for i in range(CHUNK):
                    rows[part * CHUNK + i, at, :] = kept[i].astype(jnp.float32)
                return carry

            return lax.fori_loop(0, N_DP // CHUNK, chunk, carry)

        lax.fori_loop(0, STEP // 16, tile, jnp.int32(0))

    def spread(low, carry):
        for i, distance in enumerate(places):
            p = ((my_z + distance) & (N_Z - 1)) * P_LOW + low
            at = pl.ds(pl.multiple_of((i * P_LOW + low) * GROUP_ROWS, GROUP_ROWS), GROUP_ROWS)
            for head in range(HEADS):
                weights[at, head * HS : (head + 1) * HS] = rows[
                    p, pl.ds(head, GROUP_ROWS, stride=HEADS), :
                ].astype(jnp.bfloat16)
        return carry

    def one_group(group, carry):
        def one_step(step, carry):
            for copy in copies(group * per_group + step):
                copy.wait()
            select(group, group * per_group + step)
            return carry

        lax.fori_loop(0, per_group, one_step, jnp.int32(0))
        lax.fori_loop(0, P_LOW, spread, jnp.int32(0))
        for head in range(HEADS):
            master[pl.ds(pl.multiple_of(group * GROUP_ROWS, GROUP_ROWS), GROUP_ROWS), head * HS : (head + 1) * HS] = rows[
                me, pl.ds(head, GROUP_ROWS, stride=HEADS), :
            ]
        for copy in token_copies(group):
            copy.wait()
        part = jnp.dot(columns[group], weights[...], preferred_element_type=jnp.float32)

        @pl.when(group == 0)
        def _():
            total[...] = part

        @pl.when(group > 0)
        def _():
            total[...] += part

        return carry

    lax.fori_loop(0, GROUPS, one_group, jnp.int32(0))
    cols = query.shape[1]
    query[...] = total[:, :cols].astype(query.dtype)
    key[...] = total[:, cols:].astype(key.dtype)


SMEM = pl.BlockSpec(memory_space=pltpu.SMEM)
VMEM = pl.BlockSpec(memory_space=pltpu.VMEM)


def gather_tokens(tokens, moments):
    up = [(z, (z + 1) % N_Z) for z in range(N_Z)]
    down = [(z, (z - 1) % N_Z) for z in range(N_Z)]
    half = tokens.shape[0] // 2
    from_below, from_above = tokens, tokens
    distances, arrays = [0], [tokens]
    for distance in range(1, N_Z // 2):
        from_below = lax.ppermute(from_below, "tensor", up)
        from_above = lax.ppermute(from_above, "tensor", down)
        distances += [-distance, distance]
        if distance == 3:
            from_below, from_above, moments = lax.optimization_barrier((from_below, from_above, moments))
        arrays += [from_below, from_above]
    distances.append(N_Z // 2)
    arrays.append(lax.ppermute(from_below[:half], "tensor", up))
    arrays.append(lax.ppermute(from_above[half:], "tensor", down))
    return tuple(distances), arrays, moments


def per_device(tokens, old_master, old_first, old_second, piece_lengths, piece_shifts):
    own = jnp.stack([lax.axis_index("dp"), lax.axis_index("tensor")]).astype(jnp.int32)
    depth_dev, block_cols = old_master.shape
    state = jax.ShapeDtypeStruct((depth_dev, block_cols), jnp.float32)
    slots = pltpu.VMEM((SLOTS + BUCKET, HS), jnp.float32)

    column = old_master.astype(jnp.bfloat16).reshape(SLOTS, HS)
    row = lax.all_gather(column, "dp", axis_index_groups=X_GROUPS, axis=0, tiled=True)
    gathered = lax.all_gather(row, "dp", axis_index_groups=Y_GROUPS, axis=0, tiled=True)
    gathered = gathered.reshape(NY, NC, NX, SLOTS, HS)

    tokens_dev, width = tokens.shape
    old = jnp.arange(width, dtype=jnp.int32)
    low, depth = old // depth_dev, old % depth_dev
    new = (depth // GROUP_ROWS * P_LOW + low) * GROUP_ROWS + depth % GROUP_ROWS
    order = (new[:, None] == old[None, :]).astype(jnp.bfloat16)
    ordered = jnp.dot(tokens, order, preferred_element_type=jnp.float32).astype(jnp.bfloat16)
    packed = pl.pallas_call(
        pack_kernel,
        out_shape=jax.ShapeDtypeStruct((N_DP, BUCKET, 2 * HS), jnp.bfloat16),
        in_specs=[SMEM] * 3 + [VMEM] * 2,
        out_specs=VMEM,
        scratch_shapes=[slots, slots],
        name="pack",
    )(piece_lengths, piece_shifts, own, old_first, old_second)
    received = lax.all_to_all(packed, "dp", split_axis=0, concat_axis=0, tiled=True)
    new_first, new_second = pl.pallas_call(
        unpack_kernel,
        out_shape=[state, state],
        in_specs=[SMEM] * 3 + [VMEM],
        out_specs=[VMEM] * 2,
        scratch_shapes=[slots, slots],
        name="unpack",
    )(piece_lengths, piece_shifts, own, received)

    distances, blocks, (new_first, new_second) = gather_tokens(ordered, (new_first, new_second))

    query_cols = HQ // lax.axis_size("tensor") * HS
    key_cols = block_cols - query_cols
    group_cols = P_LOW * GROUP_ROWS
    new_master, query, key = pl.pallas_call(
        functools.partial(product_kernel, distances),
        out_shape=[
            state,
            jax.ShapeDtypeStruct((tokens_dev, query_cols), jnp.bfloat16),
            jax.ShapeDtypeStruct((tokens_dev, key_cols), jnp.bfloat16),
        ],
        in_specs=[SMEM] * 3 + [pl.BlockSpec(memory_space=pl.ANY)] * (1 + len(blocks)),
        out_specs=[VMEM] * 3,
        scratch_shapes=[
            pltpu.VMEM((NY + CHUNK // (NX * NC), NX, NC, SLOTS, HS), jnp.bfloat16),
            pltpu.VMEM((GROUPS, tokens_dev, N_Z * group_cols), jnp.bfloat16),
            pltpu.VMEM((N_DP, GROUP, HS), jnp.float32),
            pltpu.VMEM((N_Z * group_cols, block_cols), jnp.bfloat16),
            pltpu.VMEM((tokens_dev, block_cols), jnp.float32),
            pltpu.SMEM((N_DP,), jnp.int32),
            pltpu.SMEM((SLOTS // 16 + 8,), jnp.int32),
            pltpu.SemaphoreType.DMA((SLOTS // STEP, 2 * NC)),
            pltpu.SemaphoreType.DMA((GROUPS, len(blocks))),
        ],
        compiler_params=pltpu.CompilerParams(vmem_limit_bytes=VMEM_LIMIT),
        cost_estimate=pl.CostEstimate(
            flops=2 * tokens_dev * width * N_Z * block_cols,
            bytes_accessed=2 * width * N_Z * (tokens_dev + block_cols),
            transcendentals=0,
        ),
        name="product",
    )(piece_lengths, piece_shifts, own, gathered, *blocks)
    return (new_master, new_first, new_second, query, key)


def solution(mesh):
    blocked = P("dp", "tensor")
    return jax.shard_map(
        per_device,
        mesh=mesh,
        in_specs=(blocked,) * 4 + (P(), P()),
        out_specs=(blocked,) * 5,
        check_vma=False,
    )
```

```python
import functools

import jax
import jax.numpy as jnp
from jax import lax
from jax.experimental import pallas as pl
from jax.experimental.pallas import tpu as pltpu
from jax.sharding import PartitionSpec as P

HQ = 48
HS = 128
NX = 4
NC = 2
HEADS = 7
ROWS = 96
SLOTS = ROWS * HEADS
HALF = SLOTS // 2
BUCKET = 16
N_DP = 64
NY = N_DP // (NX * NC)
GROUP_ROWS = 32
GROUP = GROUP_ROWS * HEADS
GROUPS = SLOTS // GROUP
STEP = 112
CHAINS = 2
CHUNK = 32
N_Z = 8
P_LOW = N_DP // N_Z
VMEM_LIMIT = 56 * 1024 * 1024


def dp_index(y, x, c):
    return (y * NX + x) * NC + c


X_GROUPS = [[dp_index(y, x, c) for x in range(NX)] for y in range(NY) for c in range(NC)]
Y_GROUPS = [[dp_index(y, x, c) for y in range(NY) for c in range(NC)] for x in range(NX)]


def pack_kernel(lengths, shifts, own, first, second, out, first_rows, second_rows):
    for rows, state in ((first_rows, first), (second_rows, second)):
        for head in range(HEADS):
            rows[pl.ds(head, ROWS, stride=HEADS), :] = state[:, head * HS : (head + 1) * HS]
        rows[SLOTS : SLOTS + BUCKET, :] = jnp.zeros((BUCKET, HS), jnp.float32)
    me = own[0]

    def piece(j, start):
        target = (me + shifts[j]) & (N_DP - 1)
        out[target, :, 0:HS] = first_rows[pl.ds(start, BUCKET), :].astype(jnp.bfloat16)
        out[target, :, HS : 2 * HS] = second_rows[pl.ds(start, BUCKET), :].astype(jnp.bfloat16)
        return start + lengths[j]

    lax.fori_loop(0, N_DP, piece, jnp.int32(0))


def unpack_kernel(lengths, shifts, own, received, first, second, first_rows, second_rows):
    me = own[0]

    def piece(j, start):
        source = (me - shifts[j]) & (N_DP - 1)
        first_rows[pl.ds(start, BUCKET), :] = received[source, :, 0:HS].astype(jnp.float32)
        second_rows[pl.ds(start, BUCKET), :] = received[source, :, HS : 2 * HS].astype(jnp.float32)
        return start + lengths[j]

    lax.fori_loop(0, N_DP, piece, jnp.int32(0))
    for rows, state in ((first_rows, first), (second_rows, second)):
        for head in range(HEADS):
            state[:, head * HS : (head + 1) * HS] = rows[pl.ds(head, ROWS, stride=HEADS), :]


def product_kernel(places, spans, lengths, shifts, own, gathered, *refs):
    tokens, (master, query, key), (held, columns, rows, weights, total, starts, firsts, sems, token_sems) = (
        refs[:-12],
        refs[-12:-9],
        refs[-9:],
    )
    me, my_z = own[0], own[1]
    blocks = held.reshape(N_DP + CHUNK, SLOTS, HS)

    def copies(step):
        slots = pl.ds(step * STEP, STEP)
        return [
            pltpu.make_async_copy(
                gathered.at[pl.ds(0, count), c, :, slots, :],
                held.at[pl.ds(at, count), :, c, slots, :],
                sems.at[step, again * NC + c],
            )
            for again, (at, count) in enumerate(((0, NY), (NY, CHUNK // (NX * NC))))
            for c in range(NC)
        ]

    def token_copies(group):
        wide = P_LOW * GROUP_ROWS
        return [
            pltpu.make_async_copy(
                block.at[:, pl.ds(group * wide, wide)],
                columns.at[group, pl.ds(row, block.shape[0]), pl.ds(column * wide, wide)],
                token_sems.at[group, i],
            )
            for i, (block, (column, row)) in enumerate(zip(tokens, spans))
        ]

    per_group = GROUP // STEP
    for group in range(GROUPS):
        for step in range(group * per_group, (group + 1) * per_group):
            for copy in copies(step):
                copy.start()
        for copy in token_copies(group):
            copy.start()

    def piece(j, start):
        starts[j] = start
        firsts[(start + 15) >> 4] = j
        return start + lengths[j]

    lax.fori_loop(0, N_DP, piece, jnp.int32(0))
    sublane = lax.broadcasted_iota(jnp.int32, (16, HS), 0).astype(jnp.int16)

    def select(group, step):
        def tile(t, carry):
            whole = step * (STEP // 16) + t
            offset = pl.multiple_of(whole * 16, 16)
            at = pl.ds(pl.multiple_of(offset - group * GROUP, 16), 16)
            begin, end = firsts[whole], firsts[whole + 1]

            def chunk(part, carry):
                def load(j):
                    base = (part * CHUNK - shifts[j]) & (N_DP - 1)
                    return [blocks[base + i, pl.ds(offset, 16), :] for i in range(CHUNK)]

                def later(j, kept):
                    take = sublane >= (starts[j] - offset).astype(jnp.int16)
                    return [jnp.where(take, new, old) for new, old in zip(load(j), kept)]

                kept = lax.fori_loop(begin + 1, end + 1, later, load(begin))
                for i in range(CHUNK):
                    rows[part * CHUNK + i, at, :] = kept[i].astype(jnp.float32)
                return carry

            return lax.fori_loop(0, N_DP // CHUNK, chunk, carry)

        lax.fori_loop(0, STEP // 16, tile, jnp.int32(0))

    def spread(low, carry):
        for i, distance in enumerate(places):
            p = ((my_z + distance) & (N_Z - 1)) * P_LOW + low
            at = pl.ds(pl.multiple_of((i * P_LOW + low) * GROUP_ROWS, GROUP_ROWS), GROUP_ROWS)
            for head in range(HEADS):
                weights[at, head * HS : (head + 1) * HS] = rows[
                    p, pl.ds(head, GROUP_ROWS, stride=HEADS), :
                ].astype(jnp.bfloat16)
        return carry

    def one_group(group, carry):
        def one_step(step, carry):
            for copy in copies(group * per_group + step):
                copy.wait()
            select(group, group * per_group + step)
            return carry

        lax.fori_loop(0, per_group, one_step, jnp.int32(0))
        lax.fori_loop(0, P_LOW, spread, jnp.int32(0))
        for head in range(HEADS):
            master[pl.ds(pl.multiple_of(group * GROUP_ROWS, GROUP_ROWS), GROUP_ROWS), head * HS : (head + 1) * HS] = rows[
                me, pl.ds(head, GROUP_ROWS, stride=HEADS), :
            ]
        for copy in token_copies(group):
            copy.wait()
        part = jnp.dot(columns[group], weights[...], preferred_element_type=jnp.float32)

        @pl.when(group == 0)
        def _():
            total[...] = part

        @pl.when(group > 0)
        def _():
            total[...] += part

        return carry

    lax.fori_loop(0, GROUPS, one_group, jnp.int32(0))
    cols = query.shape[1]
    query[...] = total[:, :cols].astype(query.dtype)
    key[...] = total[:, cols:].astype(key.dtype)


SMEM = pl.BlockSpec(memory_space=pltpu.SMEM)
VMEM = pl.BlockSpec(memory_space=pltpu.VMEM)


def gather_tokens(tokens):
    up = [(z, (z + 1) % N_Z) for z in range(N_Z)]
    down = [(z, (z - 1) % N_Z) for z in range(N_Z)]
    rows = tokens.shape[0] // CHAINS
    half = rows // 2
    distances, spans, arrays = [0], [(0, 0)], [tokens]
    for distance in range(1, N_Z // 2):
        distances += [-distance, distance]
    distances.append(N_Z // 2)
    for first in range(0, tokens.shape[0], rows):
        from_below = from_above = tokens[first : first + rows]
        for distance in range(1, N_Z // 2):
            from_below = lax.ppermute(from_below, "tensor", up)
            from_above = lax.ppermute(from_above, "tensor", down)
            spans += [(2 * distance - 1, first), (2 * distance, first)]
            arrays += [from_below, from_above]
        spans += [(N_Z - 1, first), (N_Z - 1, first + half)]
        arrays.append(lax.ppermute(from_below[:half], "tensor", up))
        arrays.append(lax.ppermute(from_above[half:], "tensor", down))
    return tuple(distances), tuple(spans), arrays


def per_device(tokens, old_master, old_first, old_second, piece_lengths, piece_shifts):
    own = jnp.stack([lax.axis_index("dp"), lax.axis_index("tensor")]).astype(jnp.int32)
    depth_dev, block_cols = old_master.shape
    state = jax.ShapeDtypeStruct((depth_dev, block_cols), jnp.float32)
    slots = pltpu.VMEM((SLOTS + BUCKET, HS), jnp.float32)

    column = old_master.astype(jnp.bfloat16).reshape(SLOTS, HS)
    row = lax.all_gather(column, "dp", axis_index_groups=X_GROUPS, axis=0, tiled=True)
    gathered = lax.all_gather(row, "dp", axis_index_groups=Y_GROUPS, axis=0, tiled=True)
    gathered = gathered.reshape(NY, NC, NX, SLOTS, HS)

    tokens_dev, width = tokens.shape
    old = jnp.arange(width, dtype=jnp.int32)
    low, depth = old // depth_dev, old % depth_dev
    new = (depth // GROUP_ROWS * P_LOW + low) * GROUP_ROWS + depth % GROUP_ROWS
    order = (new[:, None] == old[None, :]).astype(jnp.bfloat16)
    ordered = jnp.dot(tokens, order, preferred_element_type=jnp.float32).astype(jnp.bfloat16)
    packed = pl.pallas_call(
        pack_kernel,
        out_shape=jax.ShapeDtypeStruct((N_DP, BUCKET, 2 * HS), jnp.bfloat16),
        in_specs=[SMEM] * 3 + [VMEM] * 2,
        out_specs=VMEM,
        scratch_shapes=[slots, slots],
        name="pack",
    )(piece_lengths, piece_shifts, own, old_first, old_second)
    distances, spans, blocks = gather_tokens(ordered)
    ends = slice(N_Z - 1, N_Z + 1)
    packed, blocks[ends] = lax.optimization_barrier((packed, blocks[ends]))
    received = lax.all_to_all(packed, "dp", split_axis=0, concat_axis=0, tiled=True)

    query_cols = HQ // lax.axis_size("tensor") * HS
    key_cols = block_cols - query_cols
    group_cols = P_LOW * GROUP_ROWS
    new_master, query, key = pl.pallas_call(
        functools.partial(product_kernel, distances, spans),
        out_shape=[
            state,
            jax.ShapeDtypeStruct((tokens_dev, query_cols), jnp.bfloat16),
            jax.ShapeDtypeStruct((tokens_dev, key_cols), jnp.bfloat16),
        ],
        in_specs=[SMEM] * 3 + [pl.BlockSpec(memory_space=pl.ANY)] * (1 + len(blocks)),
        out_specs=[VMEM] * 3,
        scratch_shapes=[
            pltpu.VMEM((NY + CHUNK // (NX * NC), NX, NC, SLOTS, HS), jnp.bfloat16),
            pltpu.VMEM((GROUPS, tokens_dev, N_Z * group_cols), jnp.bfloat16),
            pltpu.VMEM((N_DP, GROUP, HS), jnp.float32),
            pltpu.VMEM((N_Z * group_cols, block_cols), jnp.bfloat16),
            pltpu.VMEM((tokens_dev, block_cols), jnp.float32),
            pltpu.SMEM((N_DP,), jnp.int32),
            pltpu.SMEM((SLOTS // 16 + 8,), jnp.int32),
            pltpu.SemaphoreType.DMA((SLOTS // STEP, 2 * NC)),
            pltpu.SemaphoreType.DMA((GROUPS, len(blocks))),
        ],
        compiler_params=pltpu.CompilerParams(vmem_limit_bytes=VMEM_LIMIT),
        cost_estimate=pl.CostEstimate(
            flops=2 * tokens_dev * width * N_Z * block_cols,
            bytes_accessed=2 * width * N_Z * (tokens_dev + block_cols),
            transcendentals=0,
        ),
        name="product",
    )(piece_lengths, piece_shifts, own, gathered, *blocks)
    received, key = lax.optimization_barrier((received, key))
    new_first, new_second = pl.pallas_call(
        unpack_kernel,
        out_shape=[state, state],
        in_specs=[SMEM] * 3 + [VMEM],
        out_specs=[VMEM] * 2,
        scratch_shapes=[slots, slots],
        name="unpack",
    )(piece_lengths, piece_shifts, own, received)
    return (new_master, new_first, new_second, query, key)


def solution(mesh):
    blocked = P("dp", "tensor")
    return jax.shard_map(
        per_device,
        mesh=mesh,
        in_specs=(blocked,) * 4 + (P(), P()),
        out_specs=(blocked,) * 5,
        check_vma=False,
    )
```

```python
import functools

import jax
import jax.numpy as jnp
from jax import lax
from jax.experimental import pallas as pl
from jax.experimental.pallas import tpu as pltpu
from jax.sharding import PartitionSpec as P

HQ = 48
HS = 128
NX = 4
NC = 2
HEADS = 7
ROWS = 96
SLOTS = ROWS * HEADS
HALF = SLOTS // 2
BUCKET = 16
N_DP = 64
NY = N_DP // (NX * NC)
GROUP_ROWS = 32
GROUP = GROUP_ROWS * HEADS
GROUPS = SLOTS // GROUP
STEP = 112
CHAINS = 2
CHUNK = 32
N_Z = 8
P_LOW = N_DP // N_Z
VMEM_LIMIT = 56 * 1024 * 1024


def dp_index(y, x, c):
    return (y * NX + x) * NC + c


X_GROUPS = [[dp_index(y, x, c) for x in range(NX)] for y in range(NY) for c in range(NC)]
Y_GROUPS = [[dp_index(y, x, c) for y in range(NY) for c in range(NC)] for x in range(NX)]


def pack_kernel(lengths, shifts, own, first, second, out, first_rows, second_rows):
    for rows, state in ((first_rows, first), (second_rows, second)):
        for head in range(HEADS):
            rows[pl.ds(head, ROWS, stride=HEADS), :] = state[:, head * HS : (head + 1) * HS]
        rows[SLOTS : SLOTS + BUCKET, :] = jnp.zeros((BUCKET, HS), jnp.float32)
    me = own[0]

    def piece(j, start):
        target = (me + shifts[j]) & (N_DP - 1)
        out[target, :, 0:HS] = first_rows[pl.ds(start, BUCKET), :].astype(jnp.bfloat16)
        out[target, :, HS : 2 * HS] = second_rows[pl.ds(start, BUCKET), :].astype(jnp.bfloat16)
        return start + lengths[j]

    lax.fori_loop(0, N_DP, piece, jnp.int32(0))


def unpack_kernel(lengths, shifts, own, received, first, second, first_rows, second_rows):
    me = own[0]

    def piece(j, start):
        source = (me - shifts[j]) & (N_DP - 1)
        first_rows[pl.ds(start, BUCKET), :] = received[source, :, 0:HS].astype(jnp.float32)
        second_rows[pl.ds(start, BUCKET), :] = received[source, :, HS : 2 * HS].astype(jnp.float32)
        return start + lengths[j]

    lax.fori_loop(0, N_DP, piece, jnp.int32(0))
    for rows, state in ((first_rows, first), (second_rows, second)):
        for head in range(HEADS):
            state[:, head * HS : (head + 1) * HS] = rows[pl.ds(head, ROWS, stride=HEADS), :]


def product_kernel(places, spans, lengths, shifts, own, gathered, *refs):
    tokens, (master, query, key), (held, columns, rows, weights, total, starts, firsts, sems, token_sems) = (
        refs[:-12],
        refs[-12:-9],
        refs[-9:],
    )
    me, my_z = own[0], own[1]
    blocks = held.reshape(N_DP + CHUNK, SLOTS, HS)

    def copies(step):
        slots = pl.ds(step * STEP, STEP)
        return [
            pltpu.make_async_copy(
                gathered.at[pl.ds(0, count), c, :, slots, :],
                held.at[pl.ds(at, count), :, c, slots, :],
                sems.at[step, again * NC + c],
            )
            for again, (at, count) in enumerate(((0, NY), (NY, CHUNK // (NX * NC))))
            for c in range(NC)
        ]

    def token_copies(group):
        wide = P_LOW * GROUP_ROWS
        return [
            pltpu.make_async_copy(
                block.at[:, pl.ds(group * wide, wide)],
                columns.at[group, pl.ds(row, block.shape[0]), pl.ds(column * wide, wide)],
                token_sems.at[group, i],
            )
            for i, (block, (column, row)) in enumerate(zip(tokens, spans))
        ]

    per_group = GROUP // STEP
    for group in range(GROUPS):
        for step in range(group * per_group, (group + 1) * per_group):
            for copy in copies(step):
                copy.start()
        for copy in token_copies(group):
            copy.start()

    def piece(j, start):
        starts[j] = start
        firsts[(start + 15) >> 4] = j
        return start + lengths[j]

    lax.fori_loop(0, N_DP, piece, jnp.int32(0))
    sublane = lax.broadcasted_iota(jnp.int32, (16, HS), 0).astype(jnp.int16)

    def select(group, step):
        def tile(t, carry):
            whole = step * (STEP // 16) + t
            offset = pl.multiple_of(whole * 16, 16)
            at = pl.ds(pl.multiple_of(offset - group * GROUP, 16), 16)
            begin, end = firsts[whole], firsts[whole + 1]

            def chunk(part, carry):
                def load(j):
                    base = (part * CHUNK - shifts[j]) & (N_DP - 1)
                    return [blocks[base + i, pl.ds(offset, 16), :] for i in range(CHUNK)]

                def later(j, kept):
                    take = sublane >= (starts[j] - offset).astype(jnp.int16)
                    return [jnp.where(take, new, old) for new, old in zip(load(j), kept)]

                kept = lax.fori_loop(begin + 1, end + 1, later, load(begin))
                for i in range(CHUNK):
                    rows[part * CHUNK + i, at, :] = kept[i].astype(jnp.float32)
                return carry

            return lax.fori_loop(0, N_DP // CHUNK, chunk, carry)

        lax.fori_loop(0, STEP // 16, tile, jnp.int32(0))

    def spread(low, carry):
        for i, distance in enumerate(places):
            p = ((my_z + distance) & (N_Z - 1)) * P_LOW + low
            at = pl.ds(pl.multiple_of((i * P_LOW + low) * GROUP_ROWS, GROUP_ROWS), GROUP_ROWS)
            for head in range(HEADS):
                weights[at, head * HS : (head + 1) * HS] = rows[
                    p, pl.ds(head, GROUP_ROWS, stride=HEADS), :
                ].astype(jnp.bfloat16)
        return carry

    def one_group(group, carry):
        def one_step(step, carry):
            for copy in copies(group * per_group + step):
                copy.wait()
            select(group, group * per_group + step)
            return carry

        lax.fori_loop(0, per_group, one_step, jnp.int32(0))
        lax.fori_loop(0, P_LOW, spread, jnp.int32(0))
        for head in range(HEADS):
            master[pl.ds(pl.multiple_of(group * GROUP_ROWS, GROUP_ROWS), GROUP_ROWS), head * HS : (head + 1) * HS] = rows[
                me, pl.ds(head, GROUP_ROWS, stride=HEADS), :
            ]
        for copy in token_copies(group):
            copy.wait()
        part = jnp.dot(columns[group], weights[...], preferred_element_type=jnp.float32)

        @pl.when(group == 0)
        def _():
            total[...] = part

        @pl.when(group > 0)
        def _():
            total[...] += part

        return carry

    lax.fori_loop(0, GROUPS, one_group, jnp.int32(0))
    cols = query.shape[1]
    query[...] = total[:, :cols].astype(query.dtype)
    key[...] = total[:, cols:].astype(key.dtype)


SMEM = pl.BlockSpec(memory_space=pltpu.SMEM)
VMEM = pl.BlockSpec(memory_space=pltpu.VMEM)


def gather_tokens(tokens):
    up = [(z, (z + 1) % N_Z) for z in range(N_Z)]
    down = [(z, (z - 1) % N_Z) for z in range(N_Z)]
    rows = tokens.shape[0] // CHAINS
    half = rows // 2
    distances, spans, arrays = [0], [(0, 0)], [tokens]
    for distance in range(1, N_Z // 2):
        distances += [-distance, distance]
    distances.append(N_Z // 2)
    for first in range(0, tokens.shape[0], rows):
        from_below = from_above = tokens[first : first + rows]
        for distance in range(1, N_Z // 2):
            from_below = lax.ppermute(from_below, "tensor", up)
            from_above = lax.ppermute(from_above, "tensor", down)
            spans += [(2 * distance - 1, first), (2 * distance, first)]
            arrays += [from_below, from_above]
        spans += [(N_Z - 1, first), (N_Z - 1, first + half)]
        arrays.append(lax.ppermute(from_below[:half], "tensor", up))
        arrays.append(lax.ppermute(from_above[half:], "tensor", down))
    return tuple(distances), tuple(spans), arrays


def per_device(tokens, old_master, old_first, old_second, piece_lengths, piece_shifts):
    own = jnp.stack([lax.axis_index("dp"), lax.axis_index("tensor")]).astype(jnp.int32)
    depth_dev, block_cols = old_master.shape
    state = jax.ShapeDtypeStruct((depth_dev, block_cols), jnp.float32)
    slots = pltpu.VMEM((SLOTS + BUCKET, HS), jnp.float32)

    column = old_master.astype(jnp.bfloat16).reshape(SLOTS, HS)
    row = lax.all_gather(column, "dp", axis_index_groups=X_GROUPS, axis=0, tiled=True)
    gathered = lax.all_gather(row, "dp", axis_index_groups=Y_GROUPS, axis=0, tiled=True)
    gathered = gathered.reshape(NY, NC, NX, SLOTS, HS)

    tokens_dev, width = tokens.shape
    old = jnp.arange(width, dtype=jnp.int32)
    low, depth = old // depth_dev, old % depth_dev
    new = (depth // GROUP_ROWS * P_LOW + low) * GROUP_ROWS + depth % GROUP_ROWS
    order = (new[:, None] == old[None, :]).astype(jnp.bfloat16)
    ordered = jnp.dot(tokens, order, preferred_element_type=jnp.float32).astype(jnp.bfloat16)
    packed = pl.pallas_call(
        pack_kernel,
        out_shape=jax.ShapeDtypeStruct((N_DP, BUCKET, 2 * HS), jnp.bfloat16),
        in_specs=[SMEM] * 3 + [VMEM] * 2,
        out_specs=VMEM,
        scratch_shapes=[slots, slots],
        name="pack",
    )(piece_lengths, piece_shifts, own, old_first, old_second)
    distances, spans, blocks = gather_tokens(ordered)
    packed, blocks = lax.optimization_barrier((packed, blocks))
    received = lax.all_to_all(packed, "dp", split_axis=0, concat_axis=0, tiled=True)

    query_cols = HQ // lax.axis_size("tensor") * HS
    key_cols = block_cols - query_cols
    group_cols = P_LOW * GROUP_ROWS
    new_master, query, key = pl.pallas_call(
        functools.partial(product_kernel, distances, spans),
        out_shape=[
            state,
            jax.ShapeDtypeStruct((tokens_dev, query_cols), jnp.bfloat16),
            jax.ShapeDtypeStruct((tokens_dev, key_cols), jnp.bfloat16),
        ],
        in_specs=[SMEM] * 3 + [pl.BlockSpec(memory_space=pl.ANY)] * (1 + len(blocks)),
        out_specs=[VMEM] * 3,
        scratch_shapes=[
            pltpu.VMEM((NY + CHUNK // (NX * NC), NX, NC, SLOTS, HS), jnp.bfloat16),
            pltpu.VMEM((GROUPS, tokens_dev, N_Z * group_cols), jnp.bfloat16),
            pltpu.VMEM((N_DP, GROUP, HS), jnp.float32),
            pltpu.VMEM((N_Z * group_cols, block_cols), jnp.bfloat16),
            pltpu.VMEM((tokens_dev, block_cols), jnp.float32),
            pltpu.SMEM((N_DP,), jnp.int32),
            pltpu.SMEM((SLOTS // 16 + 8,), jnp.int32),
            pltpu.SemaphoreType.DMA((SLOTS // STEP, 2 * NC)),
            pltpu.SemaphoreType.DMA((GROUPS, len(blocks))),
        ],
        compiler_params=pltpu.CompilerParams(vmem_limit_bytes=VMEM_LIMIT),
        cost_estimate=pl.CostEstimate(
            flops=2 * tokens_dev * width * N_Z * block_cols,
            bytes_accessed=2 * width * N_Z * (tokens_dev + block_cols),
            transcendentals=0,
        ),
        name="product",
    )(piece_lengths, piece_shifts, own, gathered, *blocks)
    received, key = lax.optimization_barrier((received, key))
    new_first, new_second = pl.pallas_call(
        unpack_kernel,
        out_shape=[state, state],
        in_specs=[SMEM] * 3 + [VMEM],
        out_specs=[VMEM] * 2,
        scratch_shapes=[slots, slots],
        name="unpack",
    )(piece_lengths, piece_shifts, own, received)
    return (new_master, new_first, new_second, query, key)


def solution(mesh):
    blocked = P("dp", "tensor")
    return jax.shard_map(
        per_device,
        mesh=mesh,
        in_specs=(blocked,) * 4 + (P(), P()),
        out_specs=(blocked,) * 5,
        check_vma=False,
    )
```

```python
import functools

import jax
import jax.numpy as jnp
from jax import lax
from jax.experimental import pallas as pl
from jax.experimental.pallas import tpu as pltpu
from jax.sharding import PartitionSpec as P

HQ = 48
HS = 128
NX = 4
NC = 2
HEADS = 7
ROWS = 96
SLOTS = ROWS * HEADS
HALF = SLOTS // 2
BUCKET = 16
N_DP = 64
NY = N_DP // (NX * NC)
GROUP_ROWS = 32
GROUP = GROUP_ROWS * HEADS
GROUPS = SLOTS // GROUP
STEP = 112
CHAINS = 2
TIED = 2
CHUNK = 32
N_Z = 8
P_LOW = N_DP // N_Z
VMEM_LIMIT = 56 * 1024 * 1024


def dp_index(y, x, c):
    return (y * NX + x) * NC + c


X_GROUPS = [[dp_index(y, x, c) for x in range(NX)] for y in range(NY) for c in range(NC)]
Y_GROUPS = [[dp_index(y, x, c) for y in range(NY) for c in range(NC)] for x in range(NX)]


def pack_kernel(lengths, shifts, own, first, second, out, first_rows, second_rows):
    for rows, state in ((first_rows, first), (second_rows, second)):
        for head in range(HEADS):
            rows[pl.ds(head, ROWS, stride=HEADS), :] = state[:, head * HS : (head + 1) * HS]
        rows[SLOTS : SLOTS + BUCKET, :] = jnp.zeros((BUCKET, HS), jnp.float32)
    me = own[0]

    def piece(j, start):
        target = (me + shifts[j]) & (N_DP - 1)
        out[target, :, 0:HS] = first_rows[pl.ds(start, BUCKET), :].astype(jnp.bfloat16)
        out[target, :, HS : 2 * HS] = second_rows[pl.ds(start, BUCKET), :].astype(jnp.bfloat16)
        return start + lengths[j]

    lax.fori_loop(0, N_DP, piece, jnp.int32(0))


def unpack_kernel(lengths, shifts, own, received, first, second, first_rows, second_rows):
    me = own[0]

    def piece(j, start):
        source = (me - shifts[j]) & (N_DP - 1)
        first_rows[pl.ds(start, BUCKET), :] = received[source, :, 0:HS].astype(jnp.float32)
        second_rows[pl.ds(start, BUCKET), :] = received[source, :, HS : 2 * HS].astype(jnp.float32)
        return start + lengths[j]

    lax.fori_loop(0, N_DP, piece, jnp.int32(0))
    for rows, state in ((first_rows, first), (second_rows, second)):
        for head in range(HEADS):
            state[:, head * HS : (head + 1) * HS] = rows[pl.ds(head, ROWS, stride=HEADS), :]


def product_kernel(places, spans, lengths, shifts, own, gathered, *refs):
    tokens, (master, query, key), (held, columns, rows, weights, total, starts, firsts, sems, token_sems) = (
        refs[:-12],
        refs[-12:-9],
        refs[-9:],
    )
    me, my_z = own[0], own[1]
    blocks = held.reshape(N_DP + CHUNK, SLOTS, HS)

    def copies(step):
        slots = pl.ds(step * STEP, STEP)
        return [
            pltpu.make_async_copy(
                gathered.at[pl.ds(0, count), c, :, slots, :],
                held.at[pl.ds(at, count), :, c, slots, :],
                sems.at[step, again * NC + c],
            )
            for again, (at, count) in enumerate(((0, NY), (NY, CHUNK // (NX * NC))))
            for c in range(NC)
        ]

    def token_copies(group):
        wide = P_LOW * GROUP_ROWS
        return [
            pltpu.make_async_copy(
                block.at[:, pl.ds(group * wide, wide)],
                columns.at[group, pl.ds(row, block.shape[0]), pl.ds(column * wide, wide)],
                token_sems.at[group, i],
            )
            for i, (block, (column, row)) in enumerate(zip(tokens, spans))
        ]

    per_group = GROUP // STEP
    for group in range(GROUPS):
        for step in range(group * per_group, (group + 1) * per_group):
            for copy in copies(step):
                copy.start()
        for copy in token_copies(group):
            copy.start()

    def piece(j, start):
        starts[j] = start
        firsts[(start + 15) >> 4] = j
        return start + lengths[j]

    lax.fori_loop(0, N_DP, piece, jnp.int32(0))
    sublane = lax.broadcasted_iota(jnp.int32, (16, HS), 0).astype(jnp.int16)

    def select(group, step):
        def tile(t, carry):
            whole = step * (STEP // 16) + t
            offset = pl.multiple_of(whole * 16, 16)
            at = pl.ds(pl.multiple_of(offset - group * GROUP, 16), 16)
            begin, end = firsts[whole], firsts[whole + 1]

            def chunk(part, carry):
                def load(j):
                    base = (part * CHUNK - shifts[j]) & (N_DP - 1)
                    return [blocks[base + i, pl.ds(offset, 16), :] for i in range(CHUNK)]

                def later(j, kept):
                    take = sublane >= (starts[j] - offset).astype(jnp.int16)
                    return [jnp.where(take, new, old) for new, old in zip(load(j), kept)]

                kept = lax.fori_loop(begin + 1, end + 1, later, load(begin))
                for i in range(CHUNK):
                    rows[part * CHUNK + i, at, :] = kept[i].astype(jnp.float32)
                return carry

            return lax.fori_loop(0, N_DP // CHUNK, chunk, carry)

        lax.fori_loop(0, STEP // 16, tile, jnp.int32(0))

    def spread(low, carry):
        for i, distance in enumerate(places):
            p = ((my_z + distance) & (N_Z - 1)) * P_LOW + low
            at = pl.ds(pl.multiple_of((i * P_LOW + low) * GROUP_ROWS, GROUP_ROWS), GROUP_ROWS)
            for head in range(HEADS):
                weights[at, head * HS : (head + 1) * HS] = rows[
                    p, pl.ds(head, GROUP_ROWS, stride=HEADS), :
                ].astype(jnp.bfloat16)
        return carry

    def one_group(group, carry):
        def one_step(step, carry):
            for copy in copies(group * per_group + step):
                copy.wait()
            select(group, group * per_group + step)
            return carry

        lax.fori_loop(0, per_group, one_step, jnp.int32(0))
        lax.fori_loop(0, P_LOW, spread, jnp.int32(0))
        for head in range(HEADS):
            master[pl.ds(pl.multiple_of(group * GROUP_ROWS, GROUP_ROWS), GROUP_ROWS), head * HS : (head + 1) * HS] = rows[
                me, pl.ds(head, GROUP_ROWS, stride=HEADS), :
            ]
        for copy in token_copies(group):
            copy.wait()
        part = jnp.dot(columns[group], weights[...], preferred_element_type=jnp.float32)

        @pl.when(group == 0)
        def _():
            total[...] = part

        @pl.when(group > 0)
        def _():
            total[...] += part

        return carry

    lax.fori_loop(0, GROUPS, one_group, jnp.int32(0))
    cols = query.shape[1]
    query[...] = total[:, :cols].astype(query.dtype)
    key[...] = total[:, cols:].astype(key.dtype)


SMEM = pl.BlockSpec(memory_space=pltpu.SMEM)
VMEM = pl.BlockSpec(memory_space=pltpu.VMEM)


def gather_tokens(tokens, packed):
    up = [(z, (z + 1) % N_Z) for z in range(N_Z)]
    down = [(z, (z - 1) % N_Z) for z in range(N_Z)]
    rows = tokens.shape[0] // CHAINS
    half = rows // 2
    distances, spans, arrays = [0], [(0, 0)], [tokens]
    for distance in range(1, N_Z // 2):
        distances += [-distance, distance]
    distances.append(N_Z // 2)
    for first in range(0, tokens.shape[0], rows):
        from_below = from_above = tokens[first : first + rows]
        for distance in range(1, N_Z // 2):
            from_below = lax.ppermute(from_below, "tensor", up)
            from_above = lax.ppermute(from_above, "tensor", down)
            if distance == TIED and first > 0:
                from_below, from_above, packed = lax.optimization_barrier((from_below, from_above, packed))
            spans += [(2 * distance - 1, first), (2 * distance, first)]
            arrays += [from_below, from_above]
        spans += [(N_Z - 1, first), (N_Z - 1, first + half)]
        arrays.append(lax.ppermute(from_below[:half], "tensor", up))
        arrays.append(lax.ppermute(from_above[half:], "tensor", down))
    return tuple(distances), tuple(spans), arrays, packed


def per_device(tokens, old_master, old_first, old_second, piece_lengths, piece_shifts):
    own = jnp.stack([lax.axis_index("dp"), lax.axis_index("tensor")]).astype(jnp.int32)
    depth_dev, block_cols = old_master.shape
    state = jax.ShapeDtypeStruct((depth_dev, block_cols), jnp.float32)
    slots = pltpu.VMEM((SLOTS + BUCKET, HS), jnp.float32)

    column = old_master.astype(jnp.bfloat16).reshape(SLOTS, HS)
    row = lax.all_gather(column, "dp", axis_index_groups=X_GROUPS, axis=0, tiled=True)
    gathered = lax.all_gather(row, "dp", axis_index_groups=Y_GROUPS, axis=0, tiled=True)
    gathered = gathered.reshape(NY, NC, NX, SLOTS, HS)

    tokens_dev, width = tokens.shape
    old = jnp.arange(width, dtype=jnp.int32)
    low, depth = old // depth_dev, old % depth_dev
    new = (depth // GROUP_ROWS * P_LOW + low) * GROUP_ROWS + depth % GROUP_ROWS
    order = (new[:, None] == old[None, :]).astype(jnp.bfloat16)
    ordered = jnp.dot(tokens, order, preferred_element_type=jnp.float32).astype(jnp.bfloat16)
    packed = pl.pallas_call(
        pack_kernel,
        out_shape=jax.ShapeDtypeStruct((N_DP, BUCKET, 2 * HS), jnp.bfloat16),
        in_specs=[SMEM] * 3 + [VMEM] * 2,
        out_specs=VMEM,
        scratch_shapes=[slots, slots],
        name="pack",
    )(piece_lengths, piece_shifts, own, old_first, old_second)
    distances, spans, blocks, packed = gather_tokens(ordered, packed)
    received = lax.all_to_all(packed, "dp", split_axis=0, concat_axis=0, tiled=True)

    query_cols = HQ // lax.axis_size("tensor") * HS
    key_cols = block_cols - query_cols
    group_cols = P_LOW * GROUP_ROWS
    new_master, query, key = pl.pallas_call(
        functools.partial(product_kernel, distances, spans),
        out_shape=[
            state,
            jax.ShapeDtypeStruct((tokens_dev, query_cols), jnp.bfloat16),
            jax.ShapeDtypeStruct((tokens_dev, key_cols), jnp.bfloat16),
        ],
        in_specs=[SMEM] * 3 + [pl.BlockSpec(memory_space=pl.ANY)] * (1 + len(blocks)),
        out_specs=[VMEM] * 3,
        scratch_shapes=[
            pltpu.VMEM((NY + CHUNK // (NX * NC), NX, NC, SLOTS, HS), jnp.bfloat16),
            pltpu.VMEM((GROUPS, tokens_dev, N_Z * group_cols), jnp.bfloat16),
            pltpu.VMEM((N_DP, GROUP, HS), jnp.float32),
            pltpu.VMEM((N_Z * group_cols, block_cols), jnp.bfloat16),
            pltpu.VMEM((tokens_dev, block_cols), jnp.float32),
            pltpu.SMEM((N_DP,), jnp.int32),
            pltpu.SMEM((SLOTS // 16 + 8,), jnp.int32),
            pltpu.SemaphoreType.DMA((SLOTS // STEP, 2 * NC)),
            pltpu.SemaphoreType.DMA((GROUPS, len(blocks))),
        ],
        compiler_params=pltpu.CompilerParams(vmem_limit_bytes=VMEM_LIMIT),
        cost_estimate=pl.CostEstimate(
            flops=2 * tokens_dev * width * N_Z * block_cols,
            bytes_accessed=2 * width * N_Z * (tokens_dev + block_cols),
            transcendentals=0,
        ),
        name="product",
    )(piece_lengths, piece_shifts, own, gathered, *blocks)
    received, key = lax.optimization_barrier((received, key))
    new_first, new_second = pl.pallas_call(
        unpack_kernel,
        out_shape=[state, state],
        in_specs=[SMEM] * 3 + [VMEM],
        out_specs=[VMEM] * 2,
        scratch_shapes=[slots, slots],
        name="unpack",
    )(piece_lengths, piece_shifts, own, received)
    return (new_master, new_first, new_second, query, key)


def solution(mesh):
    blocked = P("dp", "tensor")
    return jax.shard_map(
        per_device,
        mesh=mesh,
        in_specs=(blocked,) * 4 + (P(), P()),
        out_specs=(blocked,) * 5,
        check_vma=False,
    )
```
